256 devices in a mesh: inst: 32 (over x, y, core), tp: 8 (over z).
Axes of the slice: x: 4, y: 4, z: 8, core: 2. Of those that a mesh axis runs over, the one named last changes fastest.
Arguments:
- queries: bfloat16 [1024, 64, 128], P('inst', 'tp'), may hold values from -100 to 100
- new_keys: bfloat16 [1024, 8, 128], P('inst', 'tp'), may hold values from -4 to 4
- new_values: bfloat16 [1024, 8, 128], P('inst', 'tp'), may hold values from -6 to 6
- cache_keys: bfloat16 [16384, 16, 8, 128], P('inst', None, 'tp'), may hold values from -4 to 4
- cache_values: bfloat16 [16384, 16, 8, 128], P('inst', None, 'tp'), may hold values from -6 to 6
- page_table: int32 [1024, 32], P('inst'), may hold values from 0 to 511, as said below
- lengths: int32 [1024], P('inst'), may hold values from 1 to 512, 262144 in all
- remote_keys: bfloat16 [32768, 16, 8, 128], P('inst', None, 'tp'), may hold values from -4 to 4
- remote_values: bfloat16 [32768, 16, 8, 128], P('inst', None, 'tp'), may hold values from -6 to 6
- counts: int32 [32, 32], P('inst'), may hold values from 0 to 32, as said below
- page_owner: int32 [32, 32, 32], P('inst'), may hold values from 0 to 3
- query_list: int32 [32, 32, 4], P('inst'), may hold values from 0 to 31
Outputs:
- attended: bfloat16 [1024, 64, 128], P('inst', 'tp')
The draws below stay inside these ranges and needn't reach their ends.
Inputs may be any that keep to these rules, and one draw needn't show every extreme that they name: Within one instance, the first pages page_table[r, 0] of its 32 requests are distinct; other entries may repeat. `counts`: one helper, drawn from the seed, stores 32 pages for every owner instance.
All inputs are finite; a program needn't handle non-finite values. No bound on the sum of `lengths` on one device may be relied on, other than what follows from the above.
Results may differ from the reference program's by a relative error of at most 0.022.
Values may be sent and summed in bfloat16 or wider, within the bound.
A program may use at most 128 MiB of HBM per device.

```python
import math
import jax
import jax.numpy as jnp
import numpy as np
from jax import lax

QH = 64
KVH = 8
HD = 128
PAGE = 16
REQ_DEV = 32
MAXP = 32
CAP = 32
QCAP = 4
POOL = 512
INSTANCES = 32
REQS = 1024


def shared_base(key):
    return jnp.clip(jax.random.normal(key, (REQS, KVH, HD), jnp.float32), -4.0, 4.0)


def shared_table(key):
    key = jax.random.fold_in(key, 101)
    split_keys = jax.random.split(key, INSTANCES + 1)
    leading = jax.vmap(lambda sub: jax.random.permutation(sub, POOL)[:REQ_DEV])(split_keys[:INSTANCES])
    leading = leading.reshape(REQS, 1).astype(jnp.int32)
    others = jax.random.randint(split_keys[INSTANCES], (REQS, MAXP - 1), 0, POOL).astype(jnp.int32)
    return jnp.concatenate([leading, others], axis=1)


def draw_page_table(key, part):
    table = shared_table(key)
    return table


def draw_new_keys(key, part):
    base = shared_base(key)
    return base.astype(jnp.bfloat16)


def draw_queries(key, part):
    key = jax.random.fold_in(key, 5)
    first_key = jax.random.fold_in(key, 0)
    return jnp.clip(2.0 * jax.random.normal(first_key, (REQS, QH, HD), jnp.float32), -12.0, 12.0).astype(jnp.bfloat16)


def draw_cache_keys(key, part):
    key = jax.random.fold_in(key, 7)
    return jnp.clip(jax.random.normal(key, (INSTANCES * POOL, PAGE, KVH, HD), jnp.float32), -4.0, 4.0).astype(jnp.bfloat16)


def draw_counts(key, part):
    key = jax.random.fold_in(key, 3)
    first_key, second_key = jax.random.split(key)
    filled = jax.random.randint(first_key, (INSTANCES, INSTANCES), 0, CAP + 1).astype(jnp.int32)
    busiest = jax.random.randint(second_key, (), 0, INSTANCES).astype(jnp.int32)
    helper_rows = jnp.arange(INSTANCES, dtype=jnp.int32)[:, None]
    return jnp.where(helper_rows == busiest, CAP, filled).astype(jnp.int32)


def place_ends(drawn, stream_key, least, high):
    place = [jax.random.randint(jax.random.fold_in(stream_key, axis), (), 0, length) for axis, length in enumerate(drawn.shape)]
    longest = drawn.shape.index(max(drawn.shape))
    beside = place[:longest] + [(place[longest] + 1) % drawn.shape[longest]] + place[longest + 1:]
    return drawn.at[tuple(place)].set(least).at[tuple(beside)].set(high)


def levels(rng, shape, cuts, least, top_value):
    def one(position, blocks):
        steps = jax.random.uniform(jax.random.fold_in(jax.random.fold_in(rng, 6), position), (blocks,), jnp.float32, least / len(cuts), top_value / len(cuts))
        return jnp.repeat(jnp.exp(steps), shape[position] // blocks).reshape((-1,) + (1,) * (len(shape) - position - 1))

    factor_of = one(*cuts[0])
    for cut in cuts[1:]:
        factor_of = factor_of * one(*cut)
    return factor_of


def profile(number_of, total, bound, slope):
    weights = [(1 << 20) // math.isqrt(grade ** slope) + 1 for grade in range(2, number_of + 1)]
    spare, given = total - bound - (number_of - 1), [1] * (number_of - 1)
    while spare > 0:
        free = [i for i in range(number_of - 1) if given[i] < bound]
        pool, budget = sum([weights[i] for i in free]), spare
        for i in free:
            addition = min(bound - given[i], max(1, budget * weights[i] // pool), spare)
            given[i] = given[i] + addition
            spare = spare - addition
    return np.array([bound] + given)


def uneven_parts(key, amount, total, bound, skew):
    if amount == 2:
        one = jax.random.randint(key, (), max(1, total - bound), min(bound, total - 1) + 1)
        return jnp.stack([one, total - one])
    tallies = jnp.asarray(profile(amount, total, bound, skew), jnp.int32)
    pairs = (amount - 1) // 2
    giver, taker = tallies[1:1 + 2 * pairs:2], tallies[2:2 + 2 * pairs:2]
    room = jnp.minimum(giver - 1, bound - taker)
    passed = jax.random.randint(jax.random.fold_in(key, 1), (pairs,), 0, 1 << 20) % (room + 1)
    tallies = tallies.at[1:1 + 2 * pairs:2].set(giver - passed).at[2:2 + 2 * pairs:2].set(taker + passed)
    return tallies[jax.random.permutation(jax.random.fold_in(key, 2), amount)]


def scatter_about(stream_key, dims, width, bound, cuts=(), kind=jnp.bfloat16):
    gain = levels(stream_key, dims, cuts, -0.22, 0.18) if cuts else 1.0
    values = jax.random.normal(stream_key, dims, jnp.float32) * width * gain
    return jnp.minimum(jnp.maximum(values, -bound), bound).astype(kind)


def setup_inputs(seed: int = 0) -> dict:
    keys = jax.random.split(jax.random.key(seed), 13)
    queries = draw_queries(jax.random.fold_in(keys[12], 71), 0)
    new_keys = draw_new_keys(jax.random.fold_in(keys[12], 71), 0)
    new_values = scatter_about(keys[2], (REQS, KVH, HD), 1.0, 6.0, ((0, 32), (1, 8)))
    cache_keys = draw_cache_keys(jax.random.fold_in(keys[12], 71), 0)
    cache_values = scatter_about(keys[4], (INSTANCES * POOL, PAGE, KVH, HD), 1.0, 6.0, ((0, 32), (2, 8)))
    page_table = draw_page_table(jax.random.fold_in(keys[12], 71), 0)
    lengths = uneven_parts(keys[6], REQS, REQS * MAXP * PAGE // 2, MAXP * PAGE, 2).astype(jnp.int32)
    remote_keys = scatter_about(keys[7], (INSTANCES * INSTANCES * CAP, PAGE, KVH, HD), 1.0, 4.0, ((0, 32), (2, 8)))
    remote_values = scatter_about(keys[8], (INSTANCES * INSTANCES * CAP, PAGE, KVH, HD), 1.0, 6.0, ((0, 32), (2, 8)))
    counts = draw_counts(jax.random.fold_in(keys[12], 71), 0)
    page_owner = place_ends(jax.random.randint(keys[10], (INSTANCES, INSTANCES, CAP), 0, QCAP), jax.random.fold_in(keys[10], 1), 0, QCAP - 1).astype(jnp.int32)
    query_list = place_ends(jax.random.randint(keys[11], (INSTANCES, INSTANCES, QCAP), 0, REQ_DEV), jax.random.fold_in(keys[11], 1), 0, REQ_DEV - 1).astype(jnp.int32)
    return dict(queries=queries, new_keys=new_keys, new_values=new_values, cache_keys=cache_keys, cache_values=cache_values, page_table=page_table, lengths=lengths, remote_keys=remote_keys, remote_values=remote_values, counts=counts, page_owner=page_owner, query_list=query_list)


def rounded(weights):
    narrow = lax.optimization_barrier(weights.astype(jnp.bfloat16))
    return narrow.astype(jnp.float32)


def reference(queries, new_keys, new_values, cache_keys, cache_values, page_table, lengths, remote_keys, remote_values, counts, page_owner, query_list):
    group_size = QH // KVH
    score_scale = HD ** -0.5
    stored_keys = remote_keys.reshape(INSTANCES, INSTANCES, CAP * PAGE, KVH, HD)
    stored_values = remote_values.reshape(INSTANCES, INSTANCES, CAP * PAGE, KVH, HD)

    def one_instance(instance):
        first_row = (instance * REQ_DEV).astype(jnp.int32)
        query_rows = lax.dynamic_slice_in_dim(queries, first_row, REQ_DEV, 0).astype(jnp.float32)
        query_rows = query_rows.reshape(REQ_DEV, KVH, group_size, HD)
        fresh_keys = lax.dynamic_slice_in_dim(new_keys, first_row, REQ_DEV, 0).astype(jnp.float32)
        fresh_values = lax.dynamic_slice_in_dim(new_values, first_row, REQ_DEV, 0).astype(jnp.float32)
        table = lax.dynamic_slice_in_dim(page_table, first_row, REQ_DEV, 0)
        length_rows = lax.dynamic_slice_in_dim(lengths, first_row, REQ_DEV, 0)
        pool_first = (instance * POOL).astype(jnp.int32)
        pool_keys = lax.dynamic_slice_in_dim(cache_keys, pool_first, POOL, 0)
        pool_values = lax.dynamic_slice_in_dim(cache_values, pool_first, POOL, 0)
        local_keys = pool_keys[table].reshape(REQ_DEV, MAXP * PAGE, KVH, HD).astype(jnp.float32)
        local_values = pool_values[table].reshape(REQ_DEV, MAXP * PAGE, KVH, HD).astype(jnp.float32)
        live_tokens = jnp.arange(MAXP * PAGE, dtype=jnp.int32)[None, :] < length_rows[:, None]
        helper_keys = lax.dynamic_index_in_dim(stored_keys, instance, 1, False).astype(jnp.float32)
        helper_values = lax.dynamic_index_in_dim(stored_values, instance, 1, False).astype(jnp.float32)
        count_column = lax.dynamic_index_in_dim(counts, instance, 1, False)
        filled_slot = jnp.arange(CAP, dtype=jnp.int32)[None, :] < count_column[:, None]
        owners = lax.dynamic_index_in_dim(page_owner, instance, 1, False)
        slot_lists = lax.dynamic_index_in_dim(query_list, instance, 0, False)
        page_mask = (owners[:, None, :] == jnp.arange(QCAP, dtype=jnp.int32)[None, :, None]) & filled_slot[:, None, :]
        page_mask = jnp.repeat(page_mask, PAGE, axis=2)
        flat_lists = slot_lists.reshape(INSTANCES * QCAP)
        slot_queries = query_rows[slot_lists]
        new_scores = jnp.einsum("rkgd,rkd->rkg", query_rows, fresh_keys) * score_scale
        local_scores = jnp.einsum("rkgd,rtkd->rkgt", query_rows, local_keys) * score_scale
        slot_scores = jnp.einsum("aqkgd,atkd->aqkgt", slot_queries, helper_keys) * score_scale
        local_top = jnp.max(jnp.where(live_tokens[:, None, None, :], local_scores, -1e30), axis=-1)
        slot_top = jnp.max(jnp.where(page_mask[:, :, None, None, :], slot_scores, -1e30), axis=-1)
        slot_top = slot_top.reshape(INSTANCES * QCAP, KVH, group_size)
        slot_match = flat_lists[:, None] == jnp.arange(REQ_DEV, dtype=jnp.int32)[None, :]
        remote_top = jnp.max(jnp.where(slot_match[:, :, None, None], slot_top[:, None], -1e30), axis=0)
        row_peak = jnp.maximum(jnp.maximum(new_scores, local_top), remote_top)
        slot_peak = row_peak[flat_lists].reshape(INSTANCES, QCAP, KVH, group_size)
        new_weight = jnp.exp(new_scores - row_peak)
        local_weight = jnp.where(live_tokens[:, None, None, :], jnp.exp(local_scores - row_peak[..., None]), 0.0)
        slot_weight = jnp.where(page_mask[:, :, None, None, :], jnp.exp(slot_scores - slot_peak[..., None]), 0.0)
        slot_onehot = slot_match.astype(jnp.float32)
        slot_sums = jnp.sum(slot_weight, axis=-1).reshape(INSTANCES * QCAP, KVH, group_size)
        weight_sum = new_weight + jnp.sum(local_weight, axis=-1)
        weight_sum = weight_sum + jnp.einsum("sr,skg->rkg", slot_onehot, slot_sums, precision=lax.Precision.HIGHEST)
        slot_mixed = jnp.einsum("aqkgt,atkd->aqkgd", rounded(slot_weight), helper_values)
        slot_mixed = slot_mixed.reshape(INSTANCES * QCAP, KVH, group_size, HD)
        combined = rounded(new_weight)[..., None] * fresh_values[:, :, None, :]
        combined = combined + jnp.einsum("rkgt,rtkd->rkgd", rounded(local_weight), local_values)
        combined = combined + jnp.einsum("sr,skgd->rkgd", slot_onehot, slot_mixed, precision=lax.Precision.HIGHEST)
        return (combined / weight_sum[..., None]).astype(jnp.bfloat16).reshape(REQ_DEV, QH, HD)

    result = lax.map(one_instance, jnp.arange(INSTANCES, dtype=jnp.int32))
    return result.reshape(REQS, QH, HD)
```

```python
import functools
import math

import jax
import jax.numpy as jnp
from jax import lax
from jax.experimental import pallas as pl
from jax.experimental.pallas import tpu as pltpu
from jax.sharding import PartitionSpec as P

MASKED = -1e30
GROUP = 8
BLOCK = 4
EARLY = 4
STATS = 16
MESH = pl.DeviceIdType.MESH


def dot_rows(a, b):
    return lax.dot_general(a, b, (((1,), (1,)), ((), ())), preferred_element_type=jnp.float32)


def dot_plain(a, b):
    return jnp.dot(a, b, preferred_element_type=jnp.float32)


def softmax_rows(scores):
    peak = jnp.max(scores, axis=1, keepdims=True)
    weights = jnp.exp2(scores - peak)
    total = jnp.sum(weights, axis=1, keepdims=True)
    return weights.astype(jnp.bfloat16), peak + jnp.log2(total), 1.0 / total


def kernel(
    table,
    lengths,
    lists,
    counts,
    owners,
    q_hbm,
    fresh_k,
    fresh_v,
    pool_k_hbm,
    pool_v_hbm,
    store_k_hbm,
    store_v_hbm,
    out,
    q,
    q_wide,
    pool_k,
    pool_v,
    store_k,
    store_v,
    ask_out,
    ask_in,
    reply_out,
    reply_in,
    slot_of,
    row_of,
    local_out,
    local_lse,
    in_sem,
    store_sem,
    ask_send,
    ask_recv,
    reply_send,
    reply_recv,
):
    requests, _, head_dim = q_wide.shape
    group = q_wide.shape[1]
    rows = requests * group
    slots, helpers = lists.shape
    slot_rows = slots * group
    pages, page = table.shape[1], pool_k.shape[1]
    tokens = pages * page
    capacity = owners.shape[1]
    groups = helpers // GROUP
    factor = math.log2(math.e) / math.sqrt(head_dim)
    me = lax.axis_index("inst")
    mine = lax.div(me, GROUP)

    barrier = pltpu.get_barrier_semaphore()

    def greet(step, _):
        pl.semaphore_signal(
            barrier,
            inc=1,
            device_id={"inst": lax.rem(me + step, helpers)},
            device_id_type=MESH,
        )
        return 0

    q_copy = pltpu.make_async_copy(q_hbm, q, in_sem.at[0])
    q_copy.start()
    lax.fori_loop(1, helpers, greet, 0)
    pool_copies = (
        pltpu.make_async_copy(pool_k_hbm, pool_k, in_sem.at[1]),
        pltpu.make_async_copy(pool_v_hbm, pool_v, in_sem.at[2]),
    )
    for copy in pool_copies:
        copy.start()

    def store_copies(step):
        first = lax.rem(mine + step, groups) * GROUP
        span = pl.ds(first, GROUP)
        return (
            pltpu.make_async_copy(store_k_hbm.at[span], store_k.at[span], store_sem.at[0, step]),
            pltpu.make_async_copy(store_v_hbm.at[span], store_v.at[span], store_sem.at[1, step]),
        )

    for step in range(groups):
        for copy in store_copies(step):
            copy.start()

    square = (helpers, helpers)
    on_diagonal = lax.broadcasted_iota(jnp.int32, square, 0) == lax.broadcasted_iota(
        jnp.int32, square, 1
    )
    filled = jnp.where(on_diagonal, jnp.broadcast_to(counts[...], square), 0).astype(jnp.float32)
    filled = jnp.sum(filled, axis=1, keepdims=True)
    column = lax.broadcasted_iota(jnp.int32, (helpers, capacity), 1).astype(jnp.float32)
    page_slot = jnp.where(column < filled, owners[...].astype(jnp.float32), -1.0)
    spread = (
        lax.div(lax.broadcasted_iota(jnp.int32, (capacity, tokens), 1), page)
        == lax.broadcasted_iota(jnp.int32, (capacity, tokens), 0)
    ).astype(jnp.float32)
    slot_of[...] = dot_plain(page_slot.astype(jnp.bfloat16), spread.astype(jnp.bfloat16))

    lane = lax.broadcasted_iota(jnp.int32, (1, 128), 1)
    packed = 128 // slot_rows
    for part in range(helpers // packed):
        line = lax.rem(lane, group)
        for piece in range(packed * slots):
            helper, slot = part * packed + piece // slots, piece % slots
            line = jnp.where(
                lax.div(lane, group) == piece, line + lists[slot, helper] * group, line
            )
        row_of[pl.ds(part, 1), :] = line

    q_copy.wait()
    q_wide[...] = q[...].astype(jnp.float32).reshape(q_wide.shape)

    def gather(helper, _):
        picked = [q_wide[lists[slot, helper]] for slot in range(slots)]
        ask_out[helper] = jnp.concatenate(picked, axis=0).astype(jnp.bfloat16)
        return 0

    lax.fori_loop(0, helpers, gather, 0)
    ask_in[me] = ask_out[me]
    pl.semaphore_wait(barrier, helpers - 1)

    def ask(target, source):
        return pltpu.make_async_remote_copy(
            src_ref=ask_out.at[target],
            dst_ref=ask_in.at[source],
            send_sem=ask_send.at[target],
            recv_sem=ask_recv.at[source],
            device_id={"inst": target},
            device_id_type=MESH,
        )

    def reply(target, source):
        return pltpu.make_async_remote_copy(
            src_ref=reply_out.at[target],
            dst_ref=reply_in.at[source],
            send_sem=reply_send.at[target],
            recv_sem=reply_recv.at[source],
            device_id={"inst": target},
            device_id_type=MESH,
        )

    def send_ask(step, _):
        first = lax.rem(mine + groups - lax.div(step, GROUP), groups) * GROUP
        target = first + lax.rem(step, GROUP)

        @pl.when(target != me)
        def _():
            ask(target, me).start()

        return 0

    lax.fori_loop(0, helpers, send_ask, 0)

    for copy in pool_copies:
        copy.wait()
    token = lax.broadcasted_iota(jnp.int32, (group, tokens), 1)

    def local_block(block, _):
        def pages_of(pool, request):
            return jnp.concatenate([pool[table[request, j]] for j in range(pages)], axis=0)

        scores = []
        for pair in range(BLOCK // 2):
            start = pl.multiple_of(block * (BLOCK * group) + pair * 2 * group, 2 * group)
            two = q[pl.ds(start, 2 * group), :]
            for side in range(2):
                request = block * BLOCK + 2 * pair + side
                both = dot_rows(two, pages_of(pool_k, request))
                one = both[side * group : (side + 1) * group]
                scores.append(jnp.where(token < lengths[request], one * factor, MASKED))
        weights, lse, inverse = softmax_rows(jnp.concatenate(scores, axis=0))
        mixed = []
        for pair in range(BLOCK // 2):
            two = weights[pair * 2 * group : (pair + 1) * 2 * group]
            for side in range(2):
                request = block * BLOCK + 2 * pair + side
                both = dot_plain(two, pages_of(pool_v, request))
                mixed.append(both[side * group : (side + 1) * group])
        start = pl.multiple_of(block * (BLOCK * group), BLOCK * group)
        span = pl.ds(start, BLOCK * group)
        local_out[span, :] = jnp.concatenate(mixed, axis=0) * inverse
        local_lse[span, :] = jnp.broadcast_to(lse, (BLOCK * group, head_dim))
        return 0

    lax.fori_loop(0, EARLY, local_block, 0)

    wide = (slot_rows, head_dim)
    row = lax.broadcasted_iota(jnp.int32, wide, 0)
    placed = lax.broadcasted_iota(jnp.int32, wide, 1) == row + lax.rem(me, packed) * slot_rows
    row_slot = lax.div(lax.broadcasted_iota(jnp.int32, (slot_rows, tokens), 0), group).astype(
        jnp.float32
    )
    stat_row = lax.broadcasted_iota(jnp.int32, (STATS, head_dim), 0)

    def owner_group(step, _):
        first = pl.multiple_of(lax.rem(mine + step, groups) * GROUP, GROUP)
        for copy in store_copies(step):
            copy.wait()
        for j in range(GROUP):
            owner = first + j

            @pl.when(owner != me)
            def _():
                ask(me, owner).wait_recv()

        slot_lines = slot_of[pl.ds(first, GROUP), :]
        for j in range(GROUP):
            owner = first + j
            scores = dot_rows(ask_in[owner], store_k[owner]) * factor
            scores = jnp.where(slot_lines[j : j + 1] == row_slot, scores, MASKED)
            weights, lse, inverse = softmax_rows(scores)
            mixed = dot_plain(weights, store_v[owner]) * inverse
            reply_out[owner, pl.ds(0, slot_rows), :] = mixed.astype(jnp.bfloat16)
            line = jnp.sum(jnp.where(placed, lse, 0.0), axis=0, keepdims=True)
            high = line.astype(jnp.bfloat16).astype(jnp.float32)
            middle = (line - high).astype(jnp.bfloat16).astype(jnp.float32)
            low = line - high - middle
            stats = jnp.where(
                stat_row == 0,
                high,
                jnp.where(stat_row == 1, middle, jnp.where(stat_row == 2, low, 0.0)),
            )
            reply_out[owner, pl.ds(slot_rows, STATS), :] = stats.astype(jnp.bfloat16)
        for j in range(GROUP):
            owner = first + j

            @pl.when(owner != me)
            def _():
                reply(owner, me).start()

        return 0

    lax.fori_loop(0, groups, owner_group, 0)
    reply_in[me] = reply_out[me]
    lax.fori_loop(EARLY, requests // BLOCK, local_block, 0)

    def per_row(fresh):
        wide_rows = fresh[...].astype(jnp.float32)[:, None, :]
        return jnp.broadcast_to(wide_rows, (requests, group, head_dim)).reshape(rows, head_dim)

    fresh_score = jnp.sum(
        q_wide[...].reshape(rows, head_dim) * per_row(fresh_k), axis=1, keepdims=True
    )
    fresh_score = fresh_score * factor
    own_lse = local_lse[:, 0:1]

    def settle(step, _):
        other = lax.rem(me + step, helpers)
        reply(me, other).wait_recv()
        return 0

    lax.fori_loop(1, helpers, settle, 0)

    row_index = lax.broadcasted_iota(jnp.int32, (rows, 128), 0)
    parts = []
    highest = jnp.full((rows, 128), MASKED, jnp.float32)
    for part in range(helpers // packed):
        stats = reply_in[pl.ds(part * packed, packed), pl.ds(slot_rows, STATS), :]
        line = jnp.sum(jnp.sum(stats.astype(jnp.float32), axis=0), axis=0, keepdims=True)
        parts.append(line)
        match = row_of[pl.ds(part, 1), :] == row_index
        highest = jnp.maximum(highest, jnp.where(match, line, MASKED))
    peak = jnp.maximum(
        jnp.maximum(fresh_score, own_lse), jnp.max(highest, axis=1, keepdims=True)
    )
    weight_sum = jnp.zeros((rows, 128), jnp.float32)
    fresh_weight = jnp.exp2(fresh_score - peak)
    own_weight = jnp.exp2(own_lse - peak)
    total = fresh_weight * per_row(fresh_v) + own_weight * local_out[...]
    for part in range(helpers // packed):
        match = row_of[pl.ds(part, 1), :] == row_index
        weights = jnp.exp2(jnp.where(match, parts[part], MASKED) - peak)
        weight_sum = weight_sum + weights
        values = reply_in[pl.ds(part * packed, packed), pl.ds(0, slot_rows), :]
        total = total + dot_plain(weights.astype(jnp.bfloat16), values.reshape(128, head_dim))
    denominator = fresh_weight + own_weight + jnp.sum(weight_sum, axis=1, keepdims=True)
    out[...] = (total / denominator).astype(jnp.bfloat16)

    def drain(step, _):
        other = lax.rem(me + step, helpers)
        ask(other, me).wait_send()
        reply(other, me).wait_send()
        return 0

    lax.fori_loop(1, helpers, drain, 0)


def per_device(
    queries,
    new_keys,
    new_values,
    cache_keys,
    cache_values,
    page_table,
    lengths,
    remote_keys,
    remote_values,
    counts,
    page_owner,
    query_list,
):
    requests, group, head_dim = queries.shape
    helpers = lax.axis_size("inst")
    pool, page = cache_keys.shape[:2]
    capacity = remote_keys.shape[0] // helpers
    slots = query_list.shape[2]
    rows, stored = requests * group, capacity * page
    slot_rows = slots * group
    bf16, f32 = jnp.bfloat16, jnp.float32
    smem = pl.BlockSpec(memory_space=pltpu.SMEM)
    vmem = pl.BlockSpec(memory_space=pltpu.VMEM)
    anywhere = pl.BlockSpec(memory_space=pl.ANY)
    attended = pl.pallas_call(
        kernel,
        out_shape=jax.ShapeDtypeStruct((rows, head_dim), bf16),
        in_specs=[smem, smem, smem, vmem, vmem, anywhere, vmem, vmem] + [anywhere] * 4,
        out_specs=vmem,
        scratch_shapes=[
            pltpu.VMEM((rows, head_dim), bf16),
            pltpu.VMEM((requests, group, head_dim), f32),
            pltpu.VMEM((pool, page, head_dim), bf16),
            pltpu.VMEM((pool, page, head_dim), bf16),
            pltpu.VMEM((helpers, stored, head_dim), bf16),
            pltpu.VMEM((helpers, stored, head_dim), bf16),
            pltpu.VMEM((helpers, slot_rows, head_dim), bf16),
            pltpu.VMEM((helpers, slot_rows, head_dim), bf16),
            pltpu.VMEM((helpers, slot_rows + STATS, head_dim), bf16),
            pltpu.VMEM((helpers, slot_rows + STATS, head_dim), bf16),
            pltpu.VMEM((helpers, stored), f32),
            pltpu.VMEM((helpers * slot_rows // 128, 128), jnp.int32),
            pltpu.VMEM((rows, head_dim), f32),
            pltpu.VMEM((rows, head_dim), f32),
            pltpu.SemaphoreType.DMA((3,)),
            pltpu.SemaphoreType.DMA((2, helpers // GROUP)),
            pltpu.SemaphoreType.DMA((helpers,)),
            pltpu.SemaphoreType.DMA((helpers,)),
            pltpu.SemaphoreType.DMA((helpers,)),
            pltpu.SemaphoreType.DMA((helpers,)),
        ],
        compiler_params=pltpu.CompilerParams(
            collective_id=0, has_side_effects=True, vmem_limit_bytes=56 * 1024 * 1024
        ),
        cost_estimate=pl.CostEstimate(
            flops=4 * helpers * slot_rows * stored * head_dim,
            bytes_accessed=24 * helpers * stored * head_dim // 4,
            transcendentals=2 * helpers * slot_rows * stored,
        ),
    )(
        page_table,
        lengths,
        query_list[0].T,
        counts,
        page_owner[0],
        queries.reshape(rows, head_dim),
        new_keys.reshape(requests, head_dim),
        new_values.reshape(requests, head_dim),
        cache_keys.reshape(pool, page, head_dim),
        cache_values.reshape(pool, page, head_dim),
        remote_keys.reshape(helpers, stored, head_dim),
        remote_values.reshape(helpers, stored, head_dim),
    )
    return attended.reshape(requests, group, head_dim)


def solution(mesh):
    return jax.shard_map(
        per_device,
        mesh=mesh,
        in_specs=(
            P("inst", "tp", None),
            P("inst", "tp", None),
            P("inst", "tp", None),
            P("inst", None, "tp", None),
            P("inst", None, "tp", None),
            P("inst", None),
            P("inst"),
            P("inst", None, "tp", None),
            P("inst", None, "tp", None),
            P("inst", None),
            P("inst", None, None),
            P("inst", None, None),
        ),
        out_specs=P("inst", "tp", None),
        check_vma=False,
    )
```

```python
import functools
import math

import jax
import jax.numpy as jnp
from jax import lax
from jax.experimental import pallas as pl
from jax.experimental.pallas import tpu as pltpu
from jax.sharding import PartitionSpec as P

MASKED = -1e30
RING = 4
CORES = 2
GROUP = RING * CORES
FAR_FIRST = (2, 3, 1, 0)
BLOCK = 4
EARLY = 8
STATS = 16
MESH = pl.DeviceIdType.MESH


def dot_rows(a, b):
    return lax.dot_general(a, b, (((1,), (1,)), ((), ())), preferred_element_type=jnp.float32)


def dot_plain(a, b):
    return jnp.dot(a, b, preferred_element_type=jnp.float32)


def softmax_rows(scores):
    peak = jnp.max(scores, axis=1, keepdims=True)
    weights = jnp.exp2(scores - peak)
    total = jnp.sum(weights, axis=1, keepdims=True)
    return weights.astype(jnp.bfloat16), peak + jnp.log2(total), 1.0 / total


def kernel(
    table_hbm,
    lengths_hbm,
    lists_hbm,
    counts_hbm,
    owners_hbm,
    q_hbm,
    fresh_k_hbm,
    fresh_v_hbm,
    pool_k_hbm,
    pool_v_hbm,
    store_k_hbm,
    store_v_hbm,
    out,
    table,
    lengths,
    lists,
    counts,
    owners,
    fresh_k,
    fresh_v,
    q,
    q_wide,
    pool_k,
    pool_v,
    store_k,
    store_v,
    ask_out,
    ask_in,
    reply_out,
    reply_in,
    slot_of,
    row_of,
    local_out,
    local_lse,
    score,
    weight,
    in_sem,
    ask_send,
    ask_recv,
    reply_send,
    reply_recv,
):
    requests, _, head_dim = q_wide.shape
    group = q_wide.shape[1]
    rows = requests * group
    slots, helpers = lists.shape
    slot_rows = slots * group
    pages, page = table.shape[1], pool_k.shape[1]
    tokens = pages * page
    capacity = owners.shape[1]
    groups = helpers // GROUP
    factor = math.log2(math.e) / math.sqrt(head_dim)
    me = lax.axis_index("inst")
    my_x, my_y, my_core = me // GROUP, me // CORES % RING, me % CORES

    def around(step, sign):
        x_step = 2 + step - step // 2 * (2 * step - 1)
        first = (my_x + sign * x_step + RING) % RING * GROUP
        found = []
        for y_step in FAR_FIRST:
            line = first + (my_y + sign * y_step + RING) % RING * CORES
            for core_step in (1, 0):
                here = y_step == 0 and core_step == 0
                found.append((line + (my_core + core_step) % CORES, x_step != 0 if here else None))
        return found

    def others(step, sign, act):
        for device, differs in around(step, sign):
            if differs is None:
                act(device)
            else:
                pl.when(differs)(functools.partial(act, device))

    barrier = pltpu.get_barrier_semaphore()

    def greet(step, _):
        def signal(device):
            pl.semaphore_signal(
                barrier, inc=1, device_id={"inst": device}, device_id_type=MESH
            )

        others(step, 1, signal)
        return 0

    pairs = (
        (lists_hbm, lists),
        (q_hbm, q),
        (counts_hbm, counts),
        (owners_hbm, owners),
        (table_hbm, table),
        (lengths_hbm, lengths),
        (pool_k_hbm, pool_k),
        (pool_v_hbm, pool_v),
        (store_k_hbm, store_k),
        (store_v_hbm, store_v),
        (fresh_k_hbm, fresh_k),
        (fresh_v_hbm, fresh_v),
    )
    copies = [
        pltpu.make_async_copy(source, target, in_sem.at[n])
        for n, (source, target) in enumerate(pairs)
    ]
    for copy in copies[:6]:
        copy.start()
    lax.fori_loop(0, groups, greet, 0)
    for copy in copies[6:]:
        copy.start()

    for copy in copies[:2]:
        copy.wait()
    q_wide[...] = q[...].astype(jnp.float32).reshape(q_wide.shape)

    def gather(helper, _):
        picked = [q_wide[lists[slot, helper]] for slot in range(slots)]
        ask_out[helper] = jnp.concatenate(picked, axis=0).astype(jnp.bfloat16)
        return 0

    lax.fori_loop(0, helpers, gather, 0)
    ask_in[me] = ask_out[me]
    pl.semaphore_wait(barrier, helpers - 1)

    def ask(target, source):
        return pltpu.make_async_remote_copy(
            src_ref=ask_out.at[target],
            dst_ref=ask_in.at[source],
            send_sem=ask_send.at[target],
            recv_sem=ask_recv.at[source],
            device_id={"inst": target},
            device_id_type=MESH,
        )

    def reply(target, source):
        return pltpu.make_async_remote_copy(
            src_ref=reply_out.at[target],
            dst_ref=reply_in.at[source],
            send_sem=reply_send.at[target],
            recv_sem=reply_recv.at[source],
            device_id={"inst": target},
            device_id_type=MESH,
        )

    def send_ask(step, _):
        others(step, 1, lambda device: ask(device, me).start())
        return 0

    lax.fori_loop(0, groups, send_ask, 0)

    lane = lax.broadcasted_iota(jnp.int32, (1, 128), 1)
    packed = 128 // slot_rows
    for part in range(helpers // packed):
        line = lax.rem(lane, group)
        for piece in range(packed * slots):
            helper, slot = part * packed + piece // slots, piece % slots
            line = jnp.where(
                lax.div(lane, group) == piece, line + lists[slot, helper] * group, line
            )
        row_of[pl.ds(part, 1), :] = line

    for copy in copies[2:4]:
        copy.wait()
    square = (helpers, helpers)
    on_diagonal = lax.broadcasted_iota(jnp.int32, square, 0) == lax.broadcasted_iota(
        jnp.int32, square, 1
    )
    filled = jnp.where(on_diagonal, jnp.broadcast_to(counts[...], square), 0).astype(jnp.float32)
    filled = jnp.sum(filled, axis=1, keepdims=True)
    column = lax.broadcasted_iota(jnp.int32, (helpers, capacity), 1).astype(jnp.float32)
    page_slot = jnp.where(column < filled, owners[...].astype(jnp.float32), -1.0)
    spread = (
        lax.div(lax.broadcasted_iota(jnp.int32, (capacity, tokens), 1), page)
        == lax.broadcasted_iota(jnp.int32, (capacity, tokens), 0)
    ).astype(jnp.float32)
    token_slot = dot_plain(page_slot.astype(jnp.bfloat16), spread.astype(jnp.bfloat16))
    for helper in range(helpers):
        slot_of[helper] = token_slot[helper : helper + 1]

    for copy in copies[4:8]:
        copy.wait()
    token = lax.broadcasted_iota(jnp.int32, (group, tokens), 1)

    def local_block(block, _):
        def pages_of(pool, request):
            return jnp.concatenate([pool[table[request, j]] for j in range(pages)], axis=0)

        scores = []
        for pair in range(BLOCK // 2):
            start = pl.multiple_of(block * (BLOCK * group) + pair * 2 * group, 2 * group)
            two = q[pl.ds(start, 2 * group), :]
            for side in range(2):
                request = block * BLOCK + 2 * pair + side
                both = dot_rows(two, pages_of(pool_k, request))
                one = both[side * group : (side + 1) * group]
                scores.append(jnp.where(token < lengths[request], one * factor, MASKED))
        weights, lse, inverse = softmax_rows(jnp.concatenate(scores, axis=0))
        mixed = []
        for pair in range(BLOCK // 2):
            two = weights[pair * 2 * group : (pair + 1) * 2 * group]
            for side in range(2):
                request = block * BLOCK + 2 * pair + side
                both = dot_plain(two, pages_of(pool_v, request))
                mixed.append(both[side * group : (side + 1) * group])
        start = pl.multiple_of(block * (BLOCK * group), BLOCK * group)
        span = pl.ds(start, BLOCK * group)
        local_out[span, :] = jnp.concatenate(mixed, axis=0) * inverse
        local_lse[span, :] = jnp.broadcast_to(lse, (BLOCK * group, head_dim))
        return 0

    lax.fori_loop(0, EARLY, local_block, 0)

    wide = (slot_rows, head_dim)
    row = lax.broadcasted_iota(jnp.int32, wide, 0)
    placed = lax.broadcasted_iota(jnp.int32, wide, 1) == row + lax.rem(me, packed) * slot_rows
    row_slot = lax.div(lax.broadcasted_iota(jnp.int32, (slot_rows, tokens), 0), group).astype(
        jnp.float32
    )
    stat_row = lax.broadcasted_iota(jnp.int32, (STATS, head_dim), 0)

    def owner_group(step, _):
        near = [device for device, _ in around(step, -1)]
        others(step, -1, lambda device: ask(me, device).wait_recv())

        for j, owner in enumerate(near):
            score[j] = dot_rows(ask_in[owner], store_k[owner])
        scales = []
        for j, owner in enumerate(near):
            scores = jnp.where(slot_of[owner] == row_slot, score[j] * factor, MASKED)
            weights, lse, inverse = softmax_rows(scores)
            weight[j] = weights
            scales.append(inverse)
            line = jnp.sum(jnp.where(placed, lse, 0.0), axis=0, keepdims=True)
            high = line.astype(jnp.bfloat16).astype(jnp.float32)
            middle = (line - high).astype(jnp.bfloat16).astype(jnp.float32)
            low = line - high - middle
            stats = jnp.where(
                stat_row == 0,
                high,
                jnp.where(stat_row == 1, middle, jnp.where(stat_row == 2, low, 0.0)),
            )
            reply_out[owner, pl.ds(slot_rows, STATS), :] = stats.astype(jnp.bfloat16)
        for j, owner in enumerate(near):
            mixed = dot_plain(weight[j], store_v[owner]) * scales[j]
            reply_out[owner, pl.ds(0, slot_rows), :] = mixed.astype(jnp.bfloat16)
        others(step, -1, lambda device: reply(device, me).start())
        return 0

    for copy in copies[8:10]:
        copy.wait()
    lax.fori_loop(0, groups, owner_group, 0)
    reply_in[me] = reply_out[me]
    lax.fori_loop(EARLY, requests // BLOCK, local_block, 0)

    def per_row(fresh):
        wide_rows = fresh[...].astype(jnp.float32)[:, None, :]
        return jnp.broadcast_to(wide_rows, (requests, group, head_dim)).reshape(rows, head_dim)

    for copy in copies[10:]:
        copy.wait()

    fresh_score = jnp.sum(
        q_wide[...].reshape(rows, head_dim) * per_row(fresh_k), axis=1, keepdims=True
    )
    fresh_score = fresh_score * factor
    own_lse = local_lse[:, 0:1]

    def settle(step, _):
        others(step, 1, lambda device: reply(me, device).wait_recv())
        return 0

    lax.fori_loop(0, groups, settle, 0)

    row_index = lax.broadcasted_iota(jnp.int32, (rows, 128), 0)
    parts = []
    highest = jnp.full((rows, 128), MASKED, jnp.float32)
    for part in range(helpers // packed):
        stats = reply_in[pl.ds(part * packed, packed), pl.ds(slot_rows, STATS), :]
        line = jnp.sum(jnp.sum(stats.astype(jnp.float32), axis=0), axis=0, keepdims=True)
        parts.append(line)
        match = row_of[pl.ds(part, 1), :] == row_index
        highest = jnp.maximum(highest, jnp.where(match, line, MASKED))
    peak = jnp.maximum(
        jnp.maximum(fresh_score, own_lse), jnp.max(highest, axis=1, keepdims=True)
    )
    weight_sum = jnp.zeros((rows, 128), jnp.float32)
    fresh_weight = jnp.exp2(fresh_score - peak)
    own_weight = jnp.exp2(own_lse - peak)
    total = fresh_weight * per_row(fresh_v) + own_weight * local_out[...]
    for part in range(helpers // packed):
        match = row_of[pl.ds(part, 1), :] == row_index
        weights = jnp.exp2(jnp.where(match, parts[part], MASKED) - peak)
        weight_sum = weight_sum + weights
        values = reply_in[pl.ds(part * packed, packed), pl.ds(0, slot_rows), :]
        total = total + dot_plain(weights.astype(jnp.bfloat16), values.reshape(128, head_dim))
    denominator = fresh_weight + own_weight + jnp.sum(weight_sum, axis=1, keepdims=True)
    out[...] = (total / denominator).astype(jnp.bfloat16)

    def drain(step, _):
        def settled(device):
            ask(device, me).wait_send()
            reply(device, me).wait_send()

        others(step, 1, settled)
        return 0

    lax.fori_loop(0, groups, drain, 0)


def per_device(
    queries,
    new_keys,
    new_values,
    cache_keys,
    cache_values,
    page_table,
    lengths,
    remote_keys,
    remote_values,
    counts,
    page_owner,
    query_list,
):
    requests, group, head_dim = queries.shape
    helpers = lax.axis_size("inst")
    pool, page = cache_keys.shape[:2]
    capacity = remote_keys.shape[0] // helpers
    slots = query_list.shape[2]
    rows, stored = requests * group, capacity * page
    slot_rows = slots * group
    bf16, f32 = jnp.bfloat16, jnp.float32
    vmem = pl.BlockSpec(memory_space=pltpu.VMEM)
    anywhere = pl.BlockSpec(memory_space=pl.ANY)
    attended = pl.pallas_call(
        kernel,
        out_shape=pltpu.VMEM((rows, head_dim), bf16),
        in_specs=[anywhere] * 12,
        out_specs=vmem,
        scratch_shapes=[
            pltpu.SMEM(page_table.shape, jnp.int32),
            pltpu.SMEM(lengths.shape, jnp.int32),
            pltpu.SMEM((slots, helpers), jnp.int32),
            pltpu.VMEM(counts.shape, jnp.int32),
            pltpu.VMEM(page_owner.shape[1:], jnp.int32),
            pltpu.VMEM((requests, head_dim), bf16),
            pltpu.VMEM((requests, head_dim), bf16),
            pltpu.VMEM((rows, head_dim), bf16),
            pltpu.VMEM((requests, group, head_dim), f32),
            pltpu.VMEM((pool, page, head_dim), bf16),
            pltpu.VMEM((pool, page, head_dim), bf16),
            pltpu.VMEM((helpers, stored, head_dim), bf16),
            pltpu.VMEM((helpers, stored, head_dim), bf16),
            pltpu.VMEM((helpers, slot_rows, head_dim), bf16),
            pltpu.VMEM((helpers, slot_rows, head_dim), bf16),
            pltpu.VMEM((helpers, slot_rows + STATS, head_dim), bf16),
            pltpu.VMEM((helpers, slot_rows + STATS, head_dim), bf16),
            pltpu.VMEM((helpers, 1, stored), f32),
            pltpu.VMEM((helpers * slot_rows // 128, 128), jnp.int32),
            pltpu.VMEM((rows, head_dim), f32),
            pltpu.VMEM((rows, head_dim), f32),
            pltpu.VMEM((GROUP, slot_rows, stored), f32),
            pltpu.VMEM((GROUP, slot_rows, stored), bf16),
            pltpu.SemaphoreType.DMA((12,)),
            pltpu.SemaphoreType.DMA((helpers,)),
            pltpu.SemaphoreType.DMA((helpers,)),
            pltpu.SemaphoreType.DMA((helpers,)),
            pltpu.SemaphoreType.DMA((helpers,)),
        ],
        compiler_params=pltpu.CompilerParams(
            collective_id=0, has_side_effects=True, vmem_limit_bytes=56 * 1024 * 1024
        ),
        cost_estimate=pl.CostEstimate(
            flops=4 * helpers * slot_rows * stored * head_dim,
            bytes_accessed=24 * helpers * stored * head_dim // 4,
            transcendentals=2 * helpers * slot_rows * stored,
        ),
    )(
        page_table,
        lengths,
        query_list[0].T,
        counts,
        page_owner[0],
        queries.reshape(rows, head_dim),
        new_keys.reshape(requests, head_dim),
        new_values.reshape(requests, head_dim),
        cache_keys.reshape(pool, page, head_dim),
        cache_values.reshape(pool, page, head_dim),
        remote_keys.reshape(helpers, stored, head_dim),
        remote_values.reshape(helpers, stored, head_dim),
    )
    return attended.reshape(requests, group, head_dim)


def solution(mesh):
    return jax.shard_map(
        per_device,
        mesh=mesh,
        in_specs=(
            P("inst", "tp", None),
            P("inst", "tp", None),
            P("inst", "tp", None),
            P("inst", None, "tp", None),
            P("inst", None, "tp", None),
            P("inst", None),
            P("inst"),
            P("inst", None, "tp", None),
            P("inst", None, "tp", None),
            P("inst", None),
            P("inst", None, None),
            P("inst", None, None),
        ),
        out_specs=P("inst", "tp", None),
        check_vma=False,
    )
```

```python
import functools
import math

import jax
import jax.numpy as jnp
from jax import lax
from jax.experimental import pallas as pl
from jax.experimental.pallas import tpu as pltpu
from jax.sharding import PartitionSpec as P

MASKED = -1e30
RING = 4
CORES = 2
GROUP = 8
STEPS = sorted(
    ((x, y, core) for x in range(RING) for y in range(RING) for core in range(CORES)),
    key=lambda at: (-min(at[0], RING - at[0]) - min(at[1], RING - at[1]), -at[2], at),
)
BLOCK = 4
CHUNK = 256
EARLY = 4
MESH = pl.DeviceIdType.MESH


def dot_rows(a, b):
    return lax.dot_general(a, b, (((1,), (1,)), ((), ())), preferred_element_type=jnp.float32)


def dot_plain(a, b):
    return jnp.dot(a, b, preferred_element_type=jnp.float32)


def softmax_rows(scores):
    peak = jnp.max(scores, axis=1, keepdims=True)
    weights = jnp.exp2(scores - peak)
    total = jnp.sum(weights, axis=1, keepdims=True)
    return weights.astype(jnp.bfloat16), peak + jnp.log2(total), 1.0 / total


def kernel(
    table_hbm,
    lengths_hbm,
    lists_hbm,
    counts_hbm,
    owners_hbm,
    q_hbm,
    fresh_k_hbm,
    fresh_v_hbm,
    pool_k_hbm,
    pool_v_hbm,
    store_k_hbm,
    store_v_hbm,
    out,
    table,
    lengths,
    lists,
    counts,
    owners,
    fresh_k,
    fresh_v,
    q,
    q_wide,
    pool_k,
    pool_v,
    store_k,
    store_kt,
    store_v,
    ask_out,
    ask_in,
    reply_out,
    reply_in,
    stat_out,
    stat_in,
    slot_of,
    row_of,
    local_out,
    local_lse,
    score,
    weight,
    part_weight,
    in_sem,
    ask_send,
    ask_recv,
    tell_send,
    tell_recv,
    reply_send,
    reply_recv,
):
    requests, _, head_dim = q_wide.shape
    group = q_wide.shape[1]
    rows = requests * group
    slots, helpers = lists.shape
    slot_rows = slots * group
    pages, page = table.shape[1], pool_k.shape[1]
    tokens = pages * page
    capacity = owners.shape[1]
    factor = math.log2(math.e) / math.sqrt(head_dim)
    me = lax.axis_index("inst")
    my_x = lax.div(me, RING * CORES)
    my_y = lax.rem(lax.div(me, CORES), RING)
    my_core = lax.rem(me, CORES)
    planes = [lax.rem(my_x + step, RING) * (RING * CORES) for step in range(RING)]
    lines = [lax.rem(my_y + step, RING) * CORES for step in range(RING)]
    cores = (my_core, CORES - 1 - my_core)
    ahead = [planes[x] + lines[y] + cores[core] for x, y, core in STEPS]
    behind = [planes[-x % RING] + lines[-y % RING] + cores[core] for x, y, core in STEPS]

    barrier = pltpu.get_barrier_semaphore()
    for device in ahead[:-1]:
        pl.semaphore_signal(barrier, inc=1, device_id={"inst": device}, device_id_type=MESH)

    pairs = (
        (lists_hbm, lists),
        (q_hbm, q),
        (counts_hbm, counts),
        (owners_hbm, owners),
        (table_hbm, table),
        (lengths_hbm, lengths),
        (pool_k_hbm, pool_k),
        (pool_v_hbm, pool_v),
        (store_k_hbm, store_k),
        (store_v_hbm, store_v),
        (fresh_k_hbm, fresh_k),
        (fresh_v_hbm, fresh_v),
    )
    copies = [
        pltpu.make_async_copy(source, target, in_sem.at[n])
        for n, (source, target) in enumerate(pairs)
    ]
    for copy in copies:
        copy.start()

    for copy in copies[:2]:
        copy.wait()
    q_wide[...] = q[...].astype(jnp.float32).reshape(q_wide.shape)

    def gather(helper, _):
        picked = [q_wide[lists[slot, helper]] for slot in range(slots)]
        ask_out[helper] = jnp.concatenate(picked, axis=0).astype(jnp.bfloat16)
        return 0

    lax.fori_loop(0, helpers, gather, 0)
    ask_in[helpers - 1] = ask_out[me]
    pl.semaphore_wait(barrier, helpers - 1)

    def ask(place):
        return pltpu.make_async_remote_copy(
            src_ref=ask_out.at[ahead[place]],
            dst_ref=ask_in.at[place],
            send_sem=ask_send.at[place],
            recv_sem=ask_recv.at[place],
            device_id={"inst": ahead[place]},
            device_id_type=MESH,
        )

    def answer(place, out_ref, in_ref, send, recv):
        return pltpu.make_async_remote_copy(
            src_ref=out_ref.at[place],
            dst_ref=in_ref.at[place],
            send_sem=send.at[place],
            recv_sem=recv.at[place],
            device_id={"inst": behind[place]},
            device_id_type=MESH,
        )

    def tell(place):
        return answer(place, stat_out, stat_in, tell_send, tell_recv)

    def reply(place):
        return answer(place, reply_out, reply_in, reply_send, reply_recv)

    def others(start):
        return range(start, min(start + GROUP, helpers - 1))

    for place in range(helpers - 1):
        ask(place).start()

    lane = lax.broadcasted_iota(jnp.int32, (1, 128), 1)
    packed = 128 // slot_rows
    parts = helpers // packed
    for part in range(parts):
        line = lax.rem(lane, group)
        for piece in range(packed * slots):
            helper, slot = ahead[part * packed + piece // slots], piece % slots
            line = jnp.where(
                lax.div(lane, group) == piece, line + lists[slot, helper] * group, line
            )
        row_of[pl.ds(part, 1), :] = line

    for copy in copies[2:4]:
        copy.wait()
    square = (helpers, helpers)
    on_diagonal = lax.broadcasted_iota(jnp.int32, square, 0) == lax.broadcasted_iota(
        jnp.int32, square, 1
    )
    filled = jnp.where(on_diagonal, jnp.broadcast_to(counts[...], square), 0).astype(jnp.float32)
    filled = jnp.sum(filled, axis=1, keepdims=True)
    column = lax.broadcasted_iota(jnp.int32, (helpers, capacity), 1).astype(jnp.float32)
    page_slot = jnp.where(column < filled, owners[...].astype(jnp.float32), -1.0)
    spread = (
        lax.div(lax.broadcasted_iota(jnp.int32, (capacity, tokens), 1), page)
        == lax.broadcasted_iota(jnp.int32, (capacity, tokens), 0)
    ).astype(jnp.float32)
    token_slot = dot_plain(page_slot.astype(jnp.bfloat16), spread.astype(jnp.bfloat16))
    for helper in range(helpers):
        slot_of[helper] = token_slot[helper : helper + 1]

    for copy in copies[4:8]:
        copy.wait()
    token = lax.broadcasted_iota(jnp.int32, (group, tokens), 1)

    def local_block(block, _):
        def pages_of(pool, request):
            return jnp.concatenate([pool[table[request, j]] for j in range(pages)], axis=0)

        scores = []
        for pair in range(BLOCK // 2):
            start = pl.multiple_of(block * (BLOCK * group) + pair * 2 * group, 2 * group)
            two = q[pl.ds(start, 2 * group), :]
            for side in range(2):
                request = block * BLOCK + 2 * pair + side
                both = dot_rows(two, pages_of(pool_k, request))
                one = both[side * group : (side + 1) * group]
                scores.append(jnp.where(token < lengths[request], one * factor, MASKED))
        weights, lse, inverse = softmax_rows(jnp.concatenate(scores, axis=0))
        mixed = []
        for pair in range(BLOCK // 2):
            two = weights[pair * 2 * group : (pair + 1) * 2 * group]
            for side in range(2):
                request = block * BLOCK + 2 * pair + side
                both = dot_plain(two, pages_of(pool_v, request))
                mixed.append(both[side * group : (side + 1) * group])
        start = pl.multiple_of(block * (BLOCK * group), BLOCK * group)
        span = pl.ds(start, BLOCK * group)
        local_out[span, :] = jnp.concatenate(mixed, axis=0) * inverse
        local_lse[span, :] = jnp.broadcast_to(lse, (BLOCK * group, head_dim))
        return 0

    lax.fori_loop(0, EARLY, local_block, 0)

    wide = (slot_rows, head_dim)
    row = lax.broadcasted_iota(jnp.int32, wide, 0)
    offset = lax.broadcasted_iota(jnp.int32, wide, 1) - row
    placed = [offset == n * slot_rows for n in range(packed)]
    row_slot = lax.div(lax.broadcasted_iota(jnp.int32, (slot_rows, tokens), 0), group).astype(
        jnp.float32
    )

    def owner_group(start):
        near = behind[start : start + GROUP]
        for place in others(start):
            ask(place).wait_recv()
        for j, owner in enumerate(near):
            score[j] = dot_plain(ask_in[start + j], store_kt[owner])
        scales = []
        for j, owner in enumerate(near):
            scores = jnp.where(slot_of[owner] == row_slot, score[j] * factor, MASKED)
            weights, lse, inverse = softmax_rows(scores)
            weight[j] = weights
            scales.append(inverse)
            line = jnp.where(placed[(start + j) % packed], lse, 0.0)
            stat_out[start + j] = jnp.sum(line, axis=0, keepdims=True)
        for place in others(start):
            tell(place).start()
        for j, owner in enumerate(near):
            mixed = dot_plain(weight[j], store_v[owner]) * scales[j]
            reply_out[start + j] = mixed.astype(jnp.bfloat16)
        for place in others(start):
            reply(place).start()

    for copy in copies[8:10]:
        copy.wait()

    def turn(step, _):
        for j in range(4):
            store_kt[4 * step + j] = store_k[4 * step + j].T
        return 0

    lax.fori_loop(0, helpers // 4, turn, 0)
    for start in range(0, helpers, GROUP):
        owner_group(start)
    reply_in[helpers - 1] = reply_out[helpers - 1]
    stat_in[helpers - 1] = stat_out[helpers - 1]
    lax.fori_loop(EARLY, requests // BLOCK, local_block, 0)

    def per_row(fresh):
        wide_rows = fresh[...].astype(jnp.float32)[:, None, :]
        return jnp.broadcast_to(wide_rows, (requests, group, head_dim)).reshape(rows, head_dim)

    for copy in copies[10:]:
        copy.wait()

    fresh_score = jnp.sum(
        q_wide[...].reshape(rows, head_dim) * per_row(fresh_k), axis=1, keepdims=True
    )
    fresh_score = fresh_score * factor
    own_lse = local_lse[:, 0:1]
    fresh_rows = per_row(fresh_v)

    for start in range(0, helpers, GROUP):
        for place in others(start):
            tell(place).wait_recv()
    line = jnp.concatenate(
        [jnp.sum(stat_in[pl.ds(n * packed, packed)], axis=0) for n in range(parts)], axis=1
    )
    owner_row = jnp.concatenate([row_of[pl.ds(n, 1), :] for n in range(parts)], axis=1)
    for first in range(0, rows, CHUNK):
        span = slice(first, first + CHUNK)
        index = lax.broadcasted_iota(jnp.int32, (CHUNK, parts * 128), 0) + first
        lse = jnp.where(owner_row == index, line, MASKED)
        own, fresh = own_lse[span], fresh_score[span]
        peak = jnp.maximum(jnp.maximum(own, fresh), jnp.max(lse, axis=1, keepdims=True))
        weights = jnp.exp2(lse - peak)
        part_weight[span, :] = weights.astype(jnp.bfloat16)
        own, fresh = jnp.exp2(own - peak), jnp.exp2(fresh - peak)
        inverse = 1.0 / (own + fresh + jnp.sum(weights, axis=1, keepdims=True))
        local_out[span, :] = (own * local_out[span, :] + fresh * fresh_rows[span]) * inverse
        local_lse[span, :] = jnp.broadcast_to(inverse, (CHUNK, head_dim))
    for place in range(helpers - 1):
        ask(place).wait_send()
        tell(place).wait_send()
        reply(place).wait_send()
    for place in range(helpers - 1):
        reply(place).wait_recv()
    values = reply_in[...].reshape(helpers * slot_rows, head_dim)
    total = dot_plain(part_weight[...], values) * local_lse[...] + local_out[...]
    out[...] = total.astype(jnp.bfloat16)


def per_device(
    queries,
    new_keys,
    new_values,
    cache_keys,
    cache_values,
    page_table,
    lengths,
    remote_keys,
    remote_values,
    counts,
    page_owner,
    query_list,
):
    requests, group, head_dim = queries.shape
    helpers = lax.axis_size("inst")
    pool, page = cache_keys.shape[:2]
    capacity = remote_keys.shape[0] // helpers
    slots = query_list.shape[2]
    rows, stored = requests * group, capacity * page
    slot_rows = slots * group
    bf16, f32 = jnp.bfloat16, jnp.float32
    vmem = pl.BlockSpec(memory_space=pltpu.VMEM)
    anywhere = pl.BlockSpec(memory_space=pl.ANY)
    attended = pl.pallas_call(
        kernel,
        out_shape=pltpu.VMEM((rows, head_dim), bf16),
        in_specs=[anywhere] * 12,
        out_specs=vmem,
        scratch_shapes=[
            pltpu.SMEM(page_table.shape, jnp.int32),
            pltpu.SMEM(lengths.shape, jnp.int32),
            pltpu.SMEM((slots, helpers), jnp.int32),
            pltpu.VMEM(counts.shape, jnp.int32),
            pltpu.VMEM(page_owner.shape[1:], jnp.int32),
            pltpu.VMEM((requests, head_dim), bf16),
            pltpu.VMEM((requests, head_dim), bf16),
            pltpu.VMEM((rows, head_dim), bf16),
            pltpu.VMEM((requests, group, head_dim), f32),
            pltpu.VMEM((pool, page, head_dim), bf16),
            pltpu.VMEM((pool, page, head_dim), bf16),
            pltpu.VMEM((helpers, stored, head_dim), bf16),
            pltpu.VMEM((helpers, head_dim, stored), bf16),
            pltpu.VMEM((helpers, stored, head_dim), bf16),
            pltpu.VMEM((helpers, slot_rows, head_dim), bf16),
            pltpu.VMEM((helpers, slot_rows, head_dim), bf16),
            pltpu.VMEM((helpers, slot_rows, head_dim), bf16),
            pltpu.VMEM((helpers, slot_rows, head_dim), bf16),
            pltpu.VMEM((helpers, 1, 128), f32),
            pltpu.VMEM((helpers, 1, 128), f32),
            pltpu.VMEM((helpers, 1, stored), f32),
            pltpu.VMEM((helpers * slot_rows // 128, 128), jnp.int32),
            pltpu.VMEM((rows, head_dim), f32),
            pltpu.VMEM((rows, head_dim), f32),
            pltpu.VMEM((GROUP, slot_rows, stored), f32),
            pltpu.VMEM((GROUP, slot_rows, stored), bf16),
            pltpu.VMEM((rows, helpers * slot_rows), bf16),
            pltpu.SemaphoreType.DMA((12,)),
            pltpu.SemaphoreType.DMA((helpers,)),
            pltpu.SemaphoreType.DMA((helpers,)),
            pltpu.SemaphoreType.DMA((helpers,)),
            pltpu.SemaphoreType.DMA((helpers,)),
            pltpu.SemaphoreType.DMA((helpers,)),
            pltpu.SemaphoreType.DMA((helpers,)),
        ],
        compiler_params=pltpu.CompilerParams(
            collective_id=0, has_side_effects=True, vmem_limit_bytes=56 * 1024 * 1024
        ),
        cost_estimate=pl.CostEstimate(
            flops=4 * helpers * slot_rows * stored * head_dim,
            bytes_accessed=24 * helpers * stored * head_dim // 4,
            transcendentals=2 * helpers * slot_rows * stored,
        ),
    )(
        page_table,
        lengths,
        query_list[0].T,
        counts,
        page_owner[0],
        queries.reshape(rows, head_dim),
        new_keys.reshape(requests, head_dim),
        new_values.reshape(requests, head_dim),
        cache_keys.reshape(pool, page, head_dim),
        cache_values.reshape(pool, page, head_dim),
        remote_keys.reshape(helpers, stored, head_dim),
        remote_values.reshape(helpers, stored, head_dim),
    )
    return attended.reshape(requests, group, head_dim)


def solution(mesh):
    return jax.shard_map(
        per_device,
        mesh=mesh,
        in_specs=(
            P("inst", "tp", None),
            P("inst", "tp", None),
            P("inst", "tp", None),
            P("inst", None, "tp", None),
            P("inst", None, "tp", None),
            P("inst", None),
            P("inst"),
            P("inst", None, "tp", None),
            P("inst", None, "tp", None),
            P("inst", None),
            P("inst", None, None),
            P("inst", None, None),
        ),
        out_specs=P("inst", "tp", None),
        check_vma=False,
    )
```

```python
import functools
import math

import jax
import jax.numpy as jnp
from jax import lax
from jax.experimental import pallas as pl
from jax.experimental.pallas import tpu as pltpu
from jax.sharding import PartitionSpec as P

MASKED = -1e30
RING = 4
CORES = 2
BOUNDS = (0, 2, 8, 16, 24, 32)
STEPS = sorted(
    ((x, y, core) for x in range(RING) for y in range(RING) for core in range(CORES)),
    key=lambda at: (-min(at[0], RING - at[0]) - min(at[1], RING - at[1]), -at[2], at),
)
BLOCK = 4
EARLY = 4
MESH = pl.DeviceIdType.MESH


def dot_rows(a, b):
    return lax.dot_general(a, b, (((1,), (1,)), ((), ())), preferred_element_type=jnp.float32)


def dot_plain(a, b):
    return jnp.dot(a, b, preferred_element_type=jnp.float32)


def softmax_rows(scores):
    peak = jnp.max(scores, axis=1, keepdims=True)
    weights = jnp.exp2(scores - peak)
    total = jnp.sum(weights, axis=1, keepdims=True)
    return weights.astype(jnp.bfloat16), peak + jnp.log2(total), 1.0 / total


def kernel(
    table_hbm,
    lengths_hbm,
    lists_hbm,
    counts_hbm,
    owners_hbm,
    q_hbm,
    fresh_k_hbm,
    fresh_v_hbm,
    pool_k_hbm,
    pool_v_hbm,
    store_k_hbm,
    store_v_hbm,
    out,
    table,
    lengths,
    lists,
    counts,
    owners,
    fresh_k,
    fresh_v,
    q,
    q_wide,
    pool_k,
    pool_v,
    store_k,
    store_kt,
    store_v,
    ask_out,
    ask_in,
    reply_out,
    reply_in,
    stat_out,
    stat_in,
    slot_of,
    row_of,
    local_out,
    local_lse,
    score,
    weight,
    part_weight,
    in_sem,
    ask_send,
    ask_recv,
    tell_send,
    tell_recv,
    reply_send,
    reply_recv,
):
    requests, _, head_dim = q_wide.shape
    group = q_wide.shape[1]
    rows = requests * group
    slots, helpers = lists.shape
    slot_rows = slots * group
    pages, page = table.shape[1], pool_k.shape[1]
    tokens = pages * page
    capacity = owners.shape[1]
    factor = math.log2(math.e) / math.sqrt(head_dim)
    me = lax.axis_index("inst")
    my_x = lax.div(me, RING * CORES)
    my_y = lax.rem(lax.div(me, CORES), RING)
    my_core = lax.rem(me, CORES)
    planes = [lax.rem(my_x + step, RING) * (RING * CORES) for step in range(RING)]
    lines = [lax.rem(my_y + step, RING) * CORES for step in range(RING)]
    cores = (my_core, CORES - 1 - my_core)
    ahead = [planes[x] + lines[y] + cores[core] for x, y, core in STEPS]
    behind = [planes[-x % RING] + lines[-y % RING] + cores[core] for x, y, core in STEPS]

    barrier = pltpu.get_barrier_semaphore()
    for device in ahead[:-1]:
        pl.semaphore_signal(barrier, inc=1, device_id={"inst": device}, device_id_type=MESH)

    pairs = (
        (lists_hbm, lists),
        (q_hbm, q),
        (counts_hbm, counts),
        (owners_hbm, owners),
        (table_hbm, table),
        (lengths_hbm, lengths),
        (pool_k_hbm, pool_k),
        (pool_v_hbm, pool_v),
        (store_k_hbm, store_k),
        (store_v_hbm, store_v),
        (fresh_k_hbm, fresh_k),
        (fresh_v_hbm, fresh_v),
    )
    copies = [
        pltpu.make_async_copy(source, target, in_sem.at[n])
        for n, (source, target) in enumerate(pairs)
    ]
    for copy in copies:
        copy.start()

    for copy in copies[:2]:
        copy.wait()
    q_wide[...] = q[...].astype(jnp.float32).reshape(q_wide.shape)

    def gather(helper, _):
        picked = [q_wide[lists[slot, helper]] for slot in range(slots)]
        ask_out[helper] = jnp.concatenate(picked, axis=0).astype(jnp.bfloat16)
        return 0

    lax.fori_loop(0, helpers, gather, 0)
    ask_in[helpers - 1] = ask_out[me]
    pl.semaphore_wait(barrier, helpers - 1)

    def ask(place):
        return pltpu.make_async_remote_copy(
            src_ref=ask_out.at[ahead[place]],
            dst_ref=ask_in.at[place],
            send_sem=ask_send.at[place],
            recv_sem=ask_recv.at[place],
            device_id={"inst": ahead[place]},
            device_id_type=MESH,
        )

    def answer(place, out_ref, in_ref, send, recv):
        return pltpu.make_async_remote_copy(
            src_ref=out_ref.at[place],
            dst_ref=in_ref.at[place],
            send_sem=send.at[place],
            recv_sem=recv.at[place],
            device_id={"inst": behind[place]},
            device_id_type=MESH,
        )

    def tell(place):
        return answer(place, stat_out, stat_in, tell_send, tell_recv)

    def reply(place):
        return answer(place, reply_out, reply_in, reply_send, reply_recv)

    def others(start, stop):
        return range(start, min(stop, helpers - 1))

    for place in range(helpers - 1):
        ask(place).start()

    lane = lax.broadcasted_iota(jnp.int32, (1, 128), 1)
    packed = 128 // slot_rows
    parts = helpers // packed
    for part in range(parts):
        line = lax.rem(lane, group)
        for piece in range(packed * slots):
            helper, slot = ahead[part * packed + piece // slots], piece % slots
            line = jnp.where(
                lax.div(lane, group) == piece, line + lists[slot, helper] * group, line
            )
        row_of[pl.ds(part, 1), :] = line

    for copy in copies[2:4]:
        copy.wait()
    square = (helpers, helpers)
    on_diagonal = lax.broadcasted_iota(jnp.int32, square, 0) == lax.broadcasted_iota(
        jnp.int32, square, 1
    )
    filled = jnp.where(on_diagonal, jnp.broadcast_to(counts[...], square), 0).astype(jnp.float32)
    filled = jnp.sum(filled, axis=1, keepdims=True)
    column = lax.broadcasted_iota(jnp.int32, (helpers, capacity), 1).astype(jnp.float32)
    page_slot = jnp.where(column < filled, owners[...].astype(jnp.float32), -1.0)
    spread = (
        lax.div(lax.broadcasted_iota(jnp.int32, (capacity, tokens), 1), page)
        == lax.broadcasted_iota(jnp.int32, (capacity, tokens), 0)
    ).astype(jnp.float32)
    token_slot = dot_plain(page_slot.astype(jnp.bfloat16), spread.astype(jnp.bfloat16))
    for helper in range(helpers):
        slot_of[helper] = token_slot[helper : helper + 1]

    for copy in copies[4:8]:
        copy.wait()
    token = lax.broadcasted_iota(jnp.int32, (group, tokens), 1)

    def local_block(block, _):
        def pages_of(pool, request):
            return jnp.concatenate([pool[table[request, j]] for j in range(pages)], axis=0)

        scores = []
        for pair in range(BLOCK // 2):
            start = pl.multiple_of(block * (BLOCK * group) + pair * 2 * group, 2 * group)
            two = q[pl.ds(start, 2 * group), :]
            for side in range(2):
                request = block * BLOCK + 2 * pair + side
                both = dot_rows(two, pages_of(pool_k, request))
                one = both[side * group : (side + 1) * group]
                scores.append(jnp.where(token < lengths[request], one * factor, MASKED))
        weights, lse, inverse = softmax_rows(jnp.concatenate(scores, axis=0))
        mixed = []
        for pair in range(BLOCK // 2):
            two = weights[pair * 2 * group : (pair + 1) * 2 * group]
            for side in range(2):
                request = block * BLOCK + 2 * pair + side
                both = dot_plain(two, pages_of(pool_v, request))
                mixed.append(both[side * group : (side + 1) * group])
        start = pl.multiple_of(block * (BLOCK * group), BLOCK * group)
        span = pl.ds(start, BLOCK * group)
        local_out[span, :] = jnp.concatenate(mixed, axis=0) * inverse
        local_lse[span, :] = jnp.broadcast_to(lse, (BLOCK * group, head_dim))
        return 0

    lax.fori_loop(0, EARLY, local_block, 0)

    wide = (slot_rows, head_dim)
    row = lax.broadcasted_iota(jnp.int32, wide, 0)
    offset = lax.broadcasted_iota(jnp.int32, wide, 1) - row
    placed = [offset == n * slot_rows for n in range(packed)]
    row_slot = lax.div(lax.broadcasted_iota(jnp.int32, (slot_rows, tokens), 0), group).astype(
        jnp.float32
    )

    def owner_group(start, stop):
        near = behind[start:stop]
        for place in others(start, stop):
            ask(place).wait_recv()
        for j, owner in enumerate(near):
            score[j] = dot_plain(ask_in[start + j], store_kt[owner])
        scales = []
        for j, owner in enumerate(near):
            scores = jnp.where(slot_of[owner] == row_slot, score[j] * factor, MASKED)
            weights, lse, inverse = softmax_rows(scores)
            weight[j] = weights
            scales.append(inverse)
            line = jnp.where(placed[(start + j) % packed], lse, 0.0)
            stat_out[start + j] = jnp.sum(line, axis=0, keepdims=True)
        for place in others(start, stop):
            tell(place).start()
        for j, owner in enumerate(near):
            mixed = dot_plain(weight[j], store_v[owner]) * scales[j]
            reply_out[start + j] = mixed.astype(jnp.bfloat16)
        for place in others(start, stop):
            reply(place).start()

    for copy in copies[8:10]:
        copy.wait()

    def turn(step, _):
        for j in range(4):
            store_kt[4 * step + j] = store_k[4 * step + j].T
        return 0

    lax.fori_loop(0, helpers // 4, turn, 0)
    for start, stop in zip(BOUNDS, BOUNDS[1:]):
        owner_group(start, stop)
    reply_in[helpers - 1] = reply_out[helpers - 1]
    stat_in[helpers - 1] = stat_out[helpers - 1]
    lax.fori_loop(EARLY, requests // BLOCK, local_block, 0)

    def per_row(fresh):
        wide_rows = fresh[...].astype(jnp.float32)[:, None, :]
        return jnp.broadcast_to(wide_rows, (requests, group, head_dim)).reshape(rows, head_dim)

    for copy in copies[10:]:
        copy.wait()

    fresh_score = jnp.sum(
        q_wide[...].reshape(rows, head_dim) * per_row(fresh_k), axis=1, keepdims=True
    )
    fresh_score = fresh_score * factor
    own_lse = local_lse[:, 0:1]
    fresh_rows = per_row(fresh_v)

    for place in range(helpers - 1):
        tell(place).wait_recv()
    line = jnp.concatenate(
        [jnp.sum(stat_in[pl.ds(n * packed, packed)], axis=0) for n in range(parts)], axis=1
    )
    owner_row = jnp.concatenate([row_of[pl.ds(n, 1), :] for n in range(parts)], axis=1)
    index = lax.broadcasted_iota(jnp.int32, (rows, parts * 128), 0)
    lse = jnp.where(owner_row == index, line, MASKED)
    peak = jnp.maximum(
        jnp.maximum(own_lse, fresh_score), jnp.max(lse, axis=1, keepdims=True)
    )
    weights = jnp.exp2(lse - peak)
    part_weight[...] = weights.astype(jnp.bfloat16)
    own, fresh = jnp.exp2(own_lse - peak), jnp.exp2(fresh_score - peak)
    inverse = 1.0 / (own + fresh + jnp.sum(weights, axis=1, keepdims=True))
    local_out[...] = (own * local_out[...] + fresh * fresh_rows) * inverse
    local_lse[...] = jnp.broadcast_to(inverse, (rows, head_dim))
    for place in range(helpers - 1):
        ask(place).wait_send()
        tell(place).wait_send()
        reply(place).wait_send()
    for place in range(helpers - 1):
        reply(place).wait_recv()
    values = reply_in[...].reshape(helpers * slot_rows, head_dim)
    total = dot_plain(part_weight[...], values) * local_lse[...] + local_out[...]
    out[...] = total.astype(jnp.bfloat16)


def per_device(
    queries,
    new_keys,
    new_values,
    cache_keys,
    cache_values,
    page_table,
    lengths,
    remote_keys,
    remote_values,
    counts,
    page_owner,
    query_list,
):
    requests, group, head_dim = queries.shape
    helpers = lax.axis_size("inst")
    pool, page = cache_keys.shape[:2]
    capacity = remote_keys.shape[0] // helpers
    slots = query_list.shape[2]
    rows, stored = requests * group, capacity * page
    slot_rows = slots * group
    bf16, f32 = jnp.bfloat16, jnp.float32
    vmem = pl.BlockSpec(memory_space=pltpu.VMEM)
    anywhere = pl.BlockSpec(memory_space=pl.ANY)
    attended = pl.pallas_call(
        kernel,
        out_shape=pltpu.VMEM((rows, head_dim), bf16),
        in_specs=[anywhere] * 12,
        out_specs=vmem,
        scratch_shapes=[
            pltpu.SMEM(page_table.shape, jnp.int32),
            pltpu.SMEM(lengths.shape, jnp.int32),
            pltpu.SMEM((slots, helpers), jnp.int32),
            pltpu.VMEM(counts.shape, jnp.int32),
            pltpu.VMEM(page_owner.shape[1:], jnp.int32),
            pltpu.VMEM((requests, head_dim), bf16),
            pltpu.VMEM((requests, head_dim), bf16),
            pltpu.VMEM((rows, head_dim), bf16),
            pltpu.VMEM((requests, group, head_dim), f32),
            pltpu.VMEM((pool, page, head_dim), bf16),
            pltpu.VMEM((pool, page, head_dim), bf16),
            pltpu.VMEM((helpers, stored, head_dim), bf16),
            pltpu.VMEM((helpers, head_dim, stored), bf16),
            pltpu.VMEM((helpers, stored, head_dim), bf16),
            pltpu.VMEM((helpers, slot_rows, head_dim), bf16),
            pltpu.VMEM((helpers, slot_rows, head_dim), bf16),
            pltpu.VMEM((helpers, slot_rows, head_dim), bf16),
            pltpu.VMEM((helpers, slot_rows, head_dim), bf16),
            pltpu.VMEM((helpers, 1, 128), f32),
            pltpu.VMEM((helpers, 1, 128), f32),
            pltpu.VMEM((helpers, 1, stored), f32),
            pltpu.VMEM((helpers * slot_rows // 128, 128), jnp.int32),
            pltpu.VMEM((rows, head_dim), f32),
            pltpu.VMEM((rows, head_dim), f32),
            pltpu.VMEM((helpers, slot_rows, stored), f32),
            pltpu.VMEM((helpers, slot_rows, stored), bf16),
            pltpu.VMEM((rows, helpers * slot_rows), bf16),
            pltpu.SemaphoreType.DMA((12,)),
            pltpu.SemaphoreType.DMA((helpers,)),
            pltpu.SemaphoreType.DMA((helpers,)),
            pltpu.SemaphoreType.DMA((helpers,)),
            pltpu.SemaphoreType.DMA((helpers,)),
            pltpu.SemaphoreType.DMA((helpers,)),
            pltpu.SemaphoreType.DMA((helpers,)),
        ],
        compiler_params=pltpu.CompilerParams(
            collective_id=0, has_side_effects=True, vmem_limit_bytes=56 * 1024 * 1024
        ),
        cost_estimate=pl.CostEstimate(
            flops=4 * helpers * slot_rows * stored * head_dim,
            bytes_accessed=24 * helpers * stored * head_dim // 4,
            transcendentals=2 * helpers * slot_rows * stored,
        ),
    )(
        page_table,
        lengths,
        query_list[0].T,
        counts,
        page_owner[0],
        queries.reshape(rows, head_dim),
        new_keys.reshape(requests, head_dim),
        new_values.reshape(requests, head_dim),
        cache_keys.reshape(pool, page, head_dim),
        cache_values.reshape(pool, page, head_dim),
        remote_keys.reshape(helpers, stored, head_dim),
        remote_values.reshape(helpers, stored, head_dim),
    )
    return attended.reshape(requests, group, head_dim)


def solution(mesh):
    return jax.shard_map(
        per_device,
        mesh=mesh,
        in_specs=(
            P("inst", "tp", None),
            P("inst", "tp", None),
            P("inst", "tp", None),
            P("inst", None, "tp", None),
            P("inst", None, "tp", None),
            P("inst", None),
            P("inst"),
            P("inst", None, "tp", None),
            P("inst", None, "tp", None),
            P("inst", None),
            P("inst", None, None),
            P("inst", None, None),
        ),
        out_specs=P("inst", "tp", None),
        check_vma=False,
    )
```

```python
import functools
import math

import jax
import jax.numpy as jnp
from jax import lax
from jax.experimental import pallas as pl
from jax.experimental.pallas import tpu as pltpu
from jax.sharding import PartitionSpec as P

MASKED = -1e30
RING = 4
CORES = 2
BOUNDS = (0, 2, 8, 16, 24, 32)
STEPS = sorted(
    ((x, y, core) for x in range(RING) for y in range(RING) for core in range(CORES)),
    key=lambda at: (-min(at[0], RING - at[0]) - min(at[1], RING - at[1]), -at[2], at),
)
BLOCK = 4
EARLY = 3
MESH = pl.DeviceIdType.MESH


def dot_rows(a, b):
    return lax.dot_general(a, b, (((1,), (1,)), ((), ())), preferred_element_type=jnp.float32)


def dot_plain(a, b):
    return jnp.dot(a, b, preferred_element_type=jnp.float32)


def softmax_rows(scores):
    peak = jnp.max(scores, axis=1, keepdims=True)
    weights = jnp.exp2(scores - peak)
    total = jnp.sum(weights, axis=1, keepdims=True)
    return weights.astype(jnp.bfloat16), peak + jnp.log2(total), 1.0 / total


def kernel(
    table_hbm,
    lengths_hbm,
    lists_hbm,
    counts_hbm,
    owners_hbm,
    q_hbm,
    fresh_k_hbm,
    fresh_v_hbm,
    pool_k_hbm,
    pool_v_hbm,
    store_k_hbm,
    store_v_hbm,
    out,
    table,
    lengths,
    lists,
    counts,
    owners,
    fresh_k,
    fresh_v,
    q,
    q_wide,
    pool_k,
    pool_v,
    store_k,
    store_kt,
    store_v,
    ask_out,
    ask_in,
    reply_out,
    reply_in,
    stat_out,
    stat_in,
    slot_of,
    row_of,
    local_out,
    local_lse,
    score,
    weight,
    part_weight,
    in_sem,
    ask_send,
    ask_recv,
    tell_send,
    tell_recv,
    reply_send,
    reply_recv,
):
    requests, _, head_dim = q_wide.shape
    group = q_wide.shape[1]
    rows = requests * group
    slots, helpers = lists.shape
    slot_rows = slots * group
    pages, page = table.shape[1], pool_k.shape[1]
    tokens = pages * page
    capacity = owners.shape[1]
    factor = math.log2(math.e) / math.sqrt(head_dim)
    me = lax.axis_index("inst")
    my_x = lax.div(me, RING * CORES)
    my_y = lax.rem(lax.div(me, CORES), RING)
    my_core = lax.rem(me, CORES)
    planes = [lax.rem(my_x + step, RING) * (RING * CORES) for step in range(RING)]
    lines = [lax.rem(my_y + step, RING) * CORES for step in range(RING)]
    cores = (my_core, CORES - 1 - my_core)
    ahead = [planes[x] + lines[y] + cores[core] for x, y, core in STEPS]
    behind = [planes[-x % RING] + lines[-y % RING] + cores[core] for x, y, core in STEPS]

    barrier = pltpu.get_barrier_semaphore()
    for device in ahead[:-1]:
        pl.semaphore_signal(barrier, inc=1, device_id={"inst": device}, device_id_type=MESH)

    pairs = (
        (lists_hbm, lists),
        (q_hbm, q),
        (counts_hbm, counts),
        (owners_hbm, owners),
        (table_hbm, table),
        (lengths_hbm, lengths),
        (pool_k_hbm, pool_k),
        (pool_v_hbm, pool_v),
        (store_k_hbm, store_k),
        (store_v_hbm, store_v),
        (fresh_k_hbm, fresh_k),
        (fresh_v_hbm, fresh_v),
    )
    copies = [
        pltpu.make_async_copy(source, target, in_sem.at[n])
        for n, (source, target) in enumerate(pairs)
    ]
    for copy in copies:
        copy.start()

    for copy in copies[:2]:
        copy.wait()
    q_wide[...] = q[...].astype(jnp.float32).reshape(q_wide.shape)

    def gather(helper, _):
        picked = [q_wide[lists[slot, helper]] for slot in range(slots)]
        ask_out[helper] = jnp.concatenate(picked, axis=0).astype(jnp.bfloat16)
        return 0

    lax.fori_loop(0, helpers, gather, 0)
    ask_in[helpers - 1] = ask_out[me]
    pl.semaphore_wait(barrier, helpers - 1)

    def ask(place):
        return pltpu.make_async_remote_copy(
            src_ref=ask_out.at[ahead[place]],
            dst_ref=ask_in.at[place],
            send_sem=ask_send.at[place],
            recv_sem=ask_recv.at[place],
            device_id={"inst": ahead[place]},
            device_id_type=MESH,
        )

    def answer(place, out_ref, in_ref, send, recv):
        return pltpu.make_async_remote_copy(
            src_ref=out_ref.at[place],
            dst_ref=in_ref.at[place],
            send_sem=send.at[place],
            recv_sem=recv.at[place],
            device_id={"inst": behind[place]},
            device_id_type=MESH,
        )

    def tell(place):
        return answer(place, stat_out, stat_in, tell_send, tell_recv)

    def reply(place):
        return answer(place, reply_out, reply_in, reply_send, reply_recv)

    def others(start, stop):
        return range(start, min(stop, helpers - 1))

    for place in range(helpers - 1):
        ask(place).start()

    lane = lax.broadcasted_iota(jnp.int32, (1, 128), 1)
    packed = 128 // slot_rows
    parts = helpers // packed
    for part in range(parts):
        line = lax.rem(lane, group)
        for piece in range(packed * slots):
            helper, slot = ahead[part * packed + piece // slots], piece % slots
            line = jnp.where(
                lax.div(lane, group) == piece, line + lists[slot, helper] * group, line
            )
        row_of[pl.ds(part, 1), :] = line

    for copy in copies[2:4]:
        copy.wait()
    square = (helpers, helpers)
    on_diagonal = lax.broadcasted_iota(jnp.int32, square, 0) == lax.broadcasted_iota(
        jnp.int32, square, 1
    )
    filled = jnp.where(on_diagonal, jnp.broadcast_to(counts[...], square), 0).astype(jnp.float32)
    filled = jnp.sum(filled, axis=1, keepdims=True)
    column = lax.broadcasted_iota(jnp.int32, (helpers, capacity), 1).astype(jnp.float32)
    page_slot = jnp.where(column < filled, owners[...].astype(jnp.float32), -1.0)
    spread = (
        lax.div(lax.broadcasted_iota(jnp.int32, (capacity, tokens), 1), page)
        == lax.broadcasted_iota(jnp.int32, (capacity, tokens), 0)
    ).astype(jnp.float32)
    token_slot = dot_plain(page_slot.astype(jnp.bfloat16), spread.astype(jnp.bfloat16))
    for helper in range(helpers):
        slot_of[helper] = token_slot[helper : helper + 1]

    for copy in copies[4:8]:
        copy.wait()
    token = lax.broadcasted_iota(jnp.int32, (group, tokens), 1)

    def local_block(block, _):
        def pages_of(pool, request):
            return jnp.concatenate([pool[table[request, j]] for j in range(pages)], axis=0)

        scores = []
        for pair in range(BLOCK // 2):
            start = pl.multiple_of(block * (BLOCK * group) + pair * 2 * group, 2 * group)
            two = q[pl.ds(start, 2 * group), :]
            for side in range(2):
                request = block * BLOCK + 2 * pair + side
                both = dot_rows(two, pages_of(pool_k, request))
                one = both[side * group : (side + 1) * group]
                scores.append(jnp.where(token < lengths[request], one * factor, MASKED))
        weights, lse, inverse = softmax_rows(jnp.concatenate(scores, axis=0))
        mixed = []
        for pair in range(BLOCK // 2):
            two = weights[pair * 2 * group : (pair + 1) * 2 * group]
            for side in range(2):
                request = block * BLOCK + 2 * pair + side
                both = dot_plain(two, pages_of(pool_v, request))
                mixed.append(both[side * group : (side + 1) * group])
        start = pl.multiple_of(block * (BLOCK * group), BLOCK * group)
        span = pl.ds(start, BLOCK * group)
        local_out[span, :] = jnp.concatenate(mixed, axis=0) * inverse
        local_lse[span, :] = jnp.broadcast_to(lse, (BLOCK * group, head_dim))
        return 0

    lax.fori_loop(0, EARLY, local_block, 0)

    wide = (slot_rows, head_dim)
    row = lax.broadcasted_iota(jnp.int32, wide, 0)
    offset = lax.broadcasted_iota(jnp.int32, wide, 1) - row
    placed = [offset == n * slot_rows for n in range(packed)]
    row_slot = lax.div(lax.broadcasted_iota(jnp.int32, (slot_rows, tokens), 0), group).astype(
        jnp.float32
    )

    def owner_group(start, stop):
        near = behind[start:stop]
        for place in others(start, stop):
            ask(place).wait_recv()
        for j, owner in enumerate(near):
            score[j] = dot_plain(ask_in[start + j], store_kt[owner])
        scales = []
        for j, owner in enumerate(near):
            scores = jnp.where(slot_of[owner] == row_slot, score[j] * factor, MASKED)
            weights, lse, inverse = softmax_rows(scores)
            weight[j] = weights
            scales.append(inverse)
            line = jnp.where(placed[(start + j) % packed], lse, 0.0)
            stat_out[start + j] = jnp.sum(line, axis=0, keepdims=True)
        for j, owner in enumerate(near):
            mixed = dot_plain(weight[j], store_v[owner]) * scales[j]
            reply_out[start + j] = mixed.astype(jnp.bfloat16)
        for place in others(start, stop):
            tell(place).start()
        for place in others(start, stop):
            reply(place).start()

    for copy in copies[8:10]:
        copy.wait()

    def turn(step, _):
        for j in range(4):
            store_kt[4 * step + j] = store_k[4 * step + j].T
        return 0

    lax.fori_loop(0, helpers // 4, turn, 0)
    for start, stop in zip(BOUNDS, BOUNDS[1:]):
        owner_group(start, stop)
    reply_in[helpers - 1] = reply_out[helpers - 1]
    stat_in[helpers - 1] = stat_out[helpers - 1]
    lax.fori_loop(EARLY, requests // BLOCK, local_block, 0)
    for place in range(helpers - 1):
        ask(place).wait_send()
        tell(place).wait_send()
        reply(place).wait_send()

    def per_row(fresh):
        wide_rows = fresh[...].astype(jnp.float32)[:, None, :]
        return jnp.broadcast_to(wide_rows, (requests, group, head_dim)).reshape(rows, head_dim)

    for copy in copies[10:]:
        copy.wait()

    fresh_score = jnp.sum(
        q_wide[...].reshape(rows, head_dim) * per_row(fresh_k), axis=1, keepdims=True
    )
    fresh_score = fresh_score * factor
    own_lse = local_lse[:, 0:1]
    fresh_rows = per_row(fresh_v)

    for place in range(helpers - 1):
        tell(place).wait_recv()
    line = jnp.concatenate(
        [jnp.sum(stat_in[pl.ds(n * packed, packed)], axis=0) for n in range(parts)], axis=1
    )
    owner_row = jnp.concatenate([row_of[pl.ds(n, 1), :] for n in range(parts)], axis=1)
    index = lax.broadcasted_iota(jnp.int32, (rows, parts * 128), 0)
    lse = jnp.where(owner_row == index, line, MASKED)
    peak = jnp.maximum(
        jnp.maximum(own_lse, fresh_score), jnp.max(lse, axis=1, keepdims=True)
    )
    weights = jnp.exp2(lse - peak)
    part_weight[...] = weights.astype(jnp.bfloat16)
    own, fresh = jnp.exp2(own_lse - peak), jnp.exp2(fresh_score - peak)
    inverse = 1.0 / (own + fresh + jnp.sum(weights, axis=1, keepdims=True))
    local_out[...] = (own * local_out[...] + fresh * fresh_rows) * inverse
    local_lse[...] = jnp.broadcast_to(inverse, (rows, head_dim))
    for place in range(helpers - 1):
        reply(place).wait_recv()
    values = reply_in[...].reshape(helpers * slot_rows, head_dim)
    total = dot_plain(part_weight[...], values) * local_lse[...] + local_out[...]
    out[...] = total.astype(jnp.bfloat16)


def per_device(
    queries,
    new_keys,
    new_values,
    cache_keys,
    cache_values,
    page_table,
    lengths,
    remote_keys,
    remote_values,
    counts,
    page_owner,
    query_list,
):
    requests, group, head_dim = queries.shape
    helpers = lax.axis_size("inst")
    pool, page = cache_keys.shape[:2]
    capacity = remote_keys.shape[0] // helpers
    slots = query_list.shape[2]
    rows, stored = requests * group, capacity * page
    slot_rows = slots * group
    bf16, f32 = jnp.bfloat16, jnp.float32
    vmem = pl.BlockSpec(memory_space=pltpu.VMEM)
    anywhere = pl.BlockSpec(memory_space=pl.ANY)
    attended = pl.pallas_call(
        kernel,
        out_shape=pltpu.VMEM((rows, head_dim), bf16),
        in_specs=[anywhere] * 12,
        out_specs=vmem,
        scratch_shapes=[
            pltpu.SMEM(page_table.shape, jnp.int32),
            pltpu.SMEM(lengths.shape, jnp.int32),
            pltpu.SMEM((slots, helpers), jnp.int32),
            pltpu.VMEM(counts.shape, jnp.int32),
            pltpu.VMEM(page_owner.shape[1:], jnp.int32),
            pltpu.VMEM((requests, head_dim), bf16),
            pltpu.VMEM((requests, head_dim), bf16),
            pltpu.VMEM((rows, head_dim), bf16),
            pltpu.VMEM((requests, group, head_dim), f32),
            pltpu.VMEM((pool, page, head_dim), bf16),
            pltpu.VMEM((pool, page, head_dim), bf16),
            pltpu.VMEM((helpers, stored, head_dim), bf16),
            pltpu.VMEM((helpers, head_dim, stored), bf16),
            pltpu.VMEM((helpers, stored, head_dim), bf16),
            pltpu.VMEM((helpers, slot_rows, head_dim), bf16),
            pltpu.VMEM((helpers, slot_rows, head_dim), bf16),
            pltpu.VMEM((helpers, slot_rows, head_dim), bf16),
            pltpu.VMEM((helpers, slot_rows, head_dim), bf16),
            pltpu.VMEM((helpers, 1, 128), f32),
            pltpu.VMEM((helpers, 1, 128), f32),
            pltpu.VMEM((helpers, 1, stored), f32),
            pltpu.VMEM((helpers * slot_rows // 128, 128), jnp.int32),
            pltpu.VMEM((rows, head_dim), f32),
            pltpu.VMEM((rows, head_dim), f32),
            pltpu.VMEM((helpers, slot_rows, stored), f32),
            pltpu.VMEM((helpers, slot_rows, stored), bf16),
            pltpu.VMEM((rows, helpers * slot_rows), bf16),
            pltpu.SemaphoreType.DMA((12,)),
            pltpu.SemaphoreType.DMA((helpers,)),
            pltpu.SemaphoreType.DMA((helpers,)),
            pltpu.SemaphoreType.DMA((helpers,)),
            pltpu.SemaphoreType.DMA((helpers,)),
            pltpu.SemaphoreType.DMA((helpers,)),
            pltpu.SemaphoreType.DMA((helpers,)),
        ],
        compiler_params=pltpu.CompilerParams(
            collective_id=0, has_side_effects=True, vmem_limit_bytes=56 * 1024 * 1024
        ),
        cost_estimate=pl.CostEstimate(
            flops=4 * helpers * slot_rows * stored * head_dim,
            bytes_accessed=24 * helpers * stored * head_dim // 4,
            transcendentals=2 * helpers * slot_rows * stored,
        ),
    )(
        page_table,
        lengths,
        query_list[0].T,
        counts,
        page_owner[0],
        queries.reshape(rows, head_dim),
        new_keys.reshape(requests, head_dim),
        new_values.reshape(requests, head_dim),
        cache_keys.reshape(pool, page, head_dim),
        cache_values.reshape(pool, page, head_dim),
        remote_keys.reshape(helpers, stored, head_dim),
        remote_values.reshape(helpers, stored, head_dim),
    )
    return attended.reshape(requests, group, head_dim)


def solution(mesh):
    return jax.shard_map(
        per_device,
        mesh=mesh,
        in_specs=(
            P("inst", "tp", None),
            P("inst", "tp", None),
            P("inst", "tp", None),
            P("inst", None, "tp", None),
            P("inst", None, "tp", None),
            P("inst", None),
            P("inst"),
            P("inst", None, "tp", None),
            P("inst", None, "tp", None),
            P("inst", None),
            P("inst", None, None),
            P("inst", None, None),
        ),
        out_specs=P("inst", "tp", None),
        check_vma=False,
    )
```

```python
import functools
import math

import jax
import jax.numpy as jnp
from jax import lax
from jax.experimental import pallas as pl
from jax.experimental.pallas import tpu as pltpu
from jax.sharding import PartitionSpec as P

MASKED = -1e30
RING = 4
CORES = 2
BOUNDS = (0, 2, 8, 16, 24, 32)
STEPS = sorted(
    ((x, y, core) for x in range(RING) for y in range(RING) for core in range(CORES)),
    key=lambda at: (-min(at[0], RING - at[0]) - min(at[1], RING - at[1]), -at[2], at),
)
BLOCK = 4
EARLY = 3
MESH = pl.DeviceIdType.MESH


def dot_rows(a, b):
    return lax.dot_general(a, b, (((1,), (1,)), ((), ())), preferred_element_type=jnp.float32)


def dot_plain(a, b):
    return jnp.dot(a, b, preferred_element_type=jnp.float32)


def softmax_rows(scores):
    peak = jnp.max(scores, axis=1, keepdims=True)
    weights = jnp.exp2(scores - peak)
    total = jnp.sum(weights, axis=1, keepdims=True)
    return weights.astype(jnp.bfloat16), peak + jnp.log2(total), 1.0 / total


def kernel(
    table_hbm,
    lengths_hbm,
    lists_hbm,
    counts_hbm,
    owners_hbm,
    q_hbm,
    fresh_k_hbm,
    fresh_v_hbm,
    pool_k_hbm,
    pool_v_hbm,
    store_k_hbm,
    store_v_hbm,
    out,
    table,
    lengths,
    lists,
    counts,
    owners,
    fresh_k,
    fresh_v,
    q,
    q_wide,
    pool_k,
    pool_v,
    store_k,
    store_kt,
    store_v,
    ask_out,
    ask_in,
    reply_out,
    reply_in,
    stat_out,
    stat_in,
    slot_of,
    row_of,
    local_out,
    local_lse,
    score,
    weight,
    part_weight,
    in_sem,
    ask_send,
    ask_recv,
    tell_send,
    tell_recv,
    reply_send,
    reply_recv,
):
    requests, _, head_dim = q_wide.shape
    group = q_wide.shape[1]
    rows = requests * group
    slots, helpers = lists.shape
    slot_rows = slots * group
    pages, page = table.shape[1], pool_k.shape[1]
    tokens = pages * page
    capacity = owners.shape[1]
    factor = math.log2(math.e) / math.sqrt(head_dim)
    me = lax.axis_index("inst")
    my_x = lax.div(me, RING * CORES)
    my_y = lax.rem(lax.div(me, CORES), RING)
    my_core = lax.rem(me, CORES)
    planes = [lax.rem(my_x + step, RING) * (RING * CORES) for step in range(RING)]
    lines = [lax.rem(my_y + step, RING) * CORES for step in range(RING)]
    cores = (my_core, CORES - 1 - my_core)
    ahead = [planes[x] + lines[y] + cores[core] for x, y, core in STEPS]
    behind = [planes[-x % RING] + lines[-y % RING] + cores[core] for x, y, core in STEPS]

    barrier = pltpu.get_barrier_semaphore()
    for device in ahead[:-1]:
        pl.semaphore_signal(barrier, inc=1, device_id={"inst": device}, device_id_type=MESH)

    pairs = (
        (lists_hbm, lists),
        (q_hbm, q),
        (counts_hbm, counts),
        (owners_hbm, owners),
        (table_hbm, table),
        (lengths_hbm, lengths),
        (pool_k_hbm, pool_k),
        (pool_v_hbm, pool_v),
        (store_k_hbm, store_k),
        (store_v_hbm, store_v),
        (fresh_k_hbm, fresh_k),
        (fresh_v_hbm, fresh_v),
    )
    copies = [
        pltpu.make_async_copy(source, target, in_sem.at[n])
        for n, (source, target) in enumerate(pairs)
    ]
    for copy in copies:
        copy.start()

    for copy in copies[:2]:
        copy.wait()
    q_wide[...] = q[...].astype(jnp.float32).reshape(q_wide.shape)

    def gather(helper, _):
        picked = [q_wide[lists[slot, helper]] for slot in range(slots)]
        ask_out[helper] = jnp.concatenate(picked, axis=0).astype(jnp.bfloat16)
        return 0

    lax.fori_loop(0, helpers, gather, 0)
    ask_in[helpers - 1] = ask_out[me]
    lane = lax.broadcasted_iota(jnp.int32, (1, 128), 1)
    packed = 128 // slot_rows
    parts = helpers // packed
    for part in range(parts):
        line = lax.rem(lane, group)
        for piece in range(packed * slots):
            helper, slot = ahead[part * packed + piece // slots], piece % slots
            line = jnp.where(
                lax.div(lane, group) == piece, line + lists[slot, helper] * group, line
            )
        row_of[pl.ds(part, 1), :] = line

    for copy in copies[2:4]:
        copy.wait()
    square = (helpers, helpers)
    on_diagonal = lax.broadcasted_iota(jnp.int32, square, 0) == lax.broadcasted_iota(
        jnp.int32, square, 1
    )
    filled = jnp.where(on_diagonal, jnp.broadcast_to(counts[...], square), 0).astype(jnp.float32)
    filled = jnp.sum(filled, axis=1, keepdims=True)
    column = lax.broadcasted_iota(jnp.int32, (helpers, capacity), 1).astype(jnp.float32)
    page_slot = jnp.where(column < filled, owners[...].astype(jnp.float32), -1.0)
    spread = (
        lax.div(lax.broadcasted_iota(jnp.int32, (capacity, tokens), 1), page)
        == lax.broadcasted_iota(jnp.int32, (capacity, tokens), 0)
    ).astype(jnp.float32)
    token_slot = dot_plain(page_slot.astype(jnp.bfloat16), spread.astype(jnp.bfloat16))
    for helper in range(helpers):
        slot_of[helper] = token_slot[helper : helper + 1]

    pl.semaphore_wait(barrier, helpers - 1)

    def ask(place):
        return pltpu.make_async_remote_copy(
            src_ref=ask_out.at[ahead[place]],
            dst_ref=ask_in.at[place],
            send_sem=ask_send.at[place],
            recv_sem=ask_recv.at[place],
            device_id={"inst": ahead[place]},
            device_id_type=MESH,
        )

    def answer(place, out_ref, in_ref, send, recv):
        return pltpu.make_async_remote_copy(
            src_ref=out_ref.at[place],
            dst_ref=in_ref.at[place],
            send_sem=send.at[place],
            recv_sem=recv.at[place],
            device_id={"inst": behind[place]},
            device_id_type=MESH,
        )

    def tell(place):
        return answer(place, stat_out, stat_in, tell_send, tell_recv)

    def reply(place):
        return answer(place, reply_out, reply_in, reply_send, reply_recv)

    def others(start, stop):
        return range(start, min(stop, helpers - 1))

    for place in range(helpers - 1):
        ask(place).start()

    for copy in copies[4:8]:
        copy.wait()
    token = lax.broadcasted_iota(jnp.int32, (group, tokens), 1)

    def local_block(block, _):
        def pages_of(pool, request):
            return jnp.concatenate([pool[table[request, j]] for j in range(pages)], axis=0)

        scores = []
        for pair in range(BLOCK // 2):
            start = pl.multiple_of(block * (BLOCK * group) + pair * 2 * group, 2 * group)
            two = q[pl.ds(start, 2 * group), :]
            for side in range(2):
                request = block * BLOCK + 2 * pair + side
                both = dot_rows(two, pages_of(pool_k, request))
                one = both[side * group : (side + 1) * group]
                scores.append(jnp.where(token < lengths[request], one * factor, MASKED))
        weights, lse, inverse = softmax_rows(jnp.concatenate(scores, axis=0))
        mixed = []
        for pair in range(BLOCK // 2):
            two = weights[pair * 2 * group : (pair + 1) * 2 * group]
            for side in range(2):
                request = block * BLOCK + 2 * pair + side
                both = dot_plain(two, pages_of(pool_v, request))
                mixed.append(both[side * group : (side + 1) * group])
        start = pl.multiple_of(block * (BLOCK * group), BLOCK * group)
        span = pl.ds(start, BLOCK * group)
        local_out[span, :] = jnp.concatenate(mixed, axis=0) * inverse
        local_lse[span, :] = jnp.broadcast_to(lse, (BLOCK * group, head_dim))
        return 0

    lax.fori_loop(0, EARLY, local_block, 0)

    wide = (slot_rows, head_dim)
    row = lax.broadcasted_iota(jnp.int32, wide, 0)
    offset = lax.broadcasted_iota(jnp.int32, wide, 1) - row
    placed = [offset == n * slot_rows for n in range(packed)]
    row_slot = lax.div(lax.broadcasted_iota(jnp.int32, (slot_rows, tokens), 0), group).astype(
        jnp.float32
    )

    def owner_group(start, stop):
        near = behind[start:stop]
        for place in others(start, stop):
            ask(place).wait_recv()
        for j, owner in enumerate(near):
            score[j] = dot_plain(ask_in[start + j], store_kt[owner])
        scales = []
        for j, owner in enumerate(near):
            scores = jnp.where(slot_of[owner] == row_slot, score[j] * factor, MASKED)
            weights, lse, inverse = softmax_rows(scores)
            weight[j] = weights
            scales.append(inverse)
            line = jnp.where(placed[(start + j) % packed], lse, 0.0)
            stat_out[start + j] = jnp.sum(line, axis=0, keepdims=True)
        for j, owner in enumerate(near):
            mixed = dot_plain(weight[j], store_v[owner]) * scales[j]
            reply_out[start + j] = mixed.astype(jnp.bfloat16)
        for place in others(start, stop):
            tell(place).start()
        for place in others(start, stop):
            reply(place).start()

    for copy in copies[8:10]:
        copy.wait()

    def turn(step, _):
        for j in range(4):
            store_kt[4 * step + j] = store_k[4 * step + j].T
        return 0

    lax.fori_loop(0, helpers // 4, turn, 0)
    for start, stop in zip(BOUNDS, BOUNDS[1:]):
        owner_group(start, stop)
    reply_in[helpers - 1] = reply_out[helpers - 1]
    stat_in[helpers - 1] = stat_out[helpers - 1]
    lax.fori_loop(EARLY, requests // BLOCK, local_block, 0)
    for place in range(helpers - 1):
        ask(place).wait_send()
        tell(place).wait_send()
        reply(place).wait_send()

    def per_row(fresh):
        wide_rows = fresh[...].astype(jnp.float32)[:, None, :]
        return jnp.broadcast_to(wide_rows, (requests, group, head_dim)).reshape(rows, head_dim)

    for copy in copies[10:]:
        copy.wait()

    fresh_score = jnp.sum(
        q_wide[...].reshape(rows, head_dim) * per_row(fresh_k), axis=1, keepdims=True
    )
    fresh_score = fresh_score * factor
    own_lse = local_lse[:, 0:1]
    fresh_rows = per_row(fresh_v)

    for place in range(helpers - 1):
        tell(place).wait_recv()
    line = jnp.concatenate(
        [jnp.sum(stat_in[pl.ds(n * packed, packed)], axis=0) for n in range(parts)], axis=1
    )
    owner_row = jnp.concatenate([row_of[pl.ds(n, 1), :] for n in range(parts)], axis=1)
    index = lax.broadcasted_iota(jnp.int32, (rows, parts * 128), 0)
    lse = jnp.where(owner_row == index, line, MASKED)
    peak = jnp.maximum(
        jnp.maximum(own_lse, fresh_score), jnp.max(lse, axis=1, keepdims=True)
    )
    weights = jnp.exp2(lse - peak)
    part_weight[...] = weights.astype(jnp.bfloat16)
    own, fresh = jnp.exp2(own_lse - peak), jnp.exp2(fresh_score - peak)
    inverse = 1.0 / (own + fresh + jnp.sum(weights, axis=1, keepdims=True))
    local_out[...] = (own * local_out[...] + fresh * fresh_rows) * inverse
    local_lse[...] = jnp.broadcast_to(inverse, (rows, head_dim))
    for place in range(helpers - 1):
        reply(place).wait_recv()
    values = reply_in[...].reshape(helpers * slot_rows, head_dim)
    total = dot_plain(part_weight[...], values) * local_lse[...] + local_out[...]
    out[...] = total.astype(jnp.bfloat16)


def per_device(
    queries,
    new_keys,
    new_values,
    cache_keys,
    cache_values,
    page_table,
    lengths,
    remote_keys,
    remote_values,
    counts,
    page_owner,
    query_list,
):
    requests, group, head_dim = queries.shape
    helpers = lax.axis_size("inst")
    pool, page = cache_keys.shape[:2]
    capacity = remote_keys.shape[0] // helpers
    slots = query_list.shape[2]
    rows, stored = requests * group, capacity * page
    slot_rows = slots * group
    bf16, f32 = jnp.bfloat16, jnp.float32
    vmem = pl.BlockSpec(memory_space=pltpu.VMEM)
    anywhere = pl.BlockSpec(memory_space=pl.ANY)
    attended = pl.pallas_call(
        kernel,
        out_shape=pltpu.VMEM((rows, head_dim), bf16),
        in_specs=[anywhere] * 12,
        out_specs=vmem,
        scratch_shapes=[
            pltpu.SMEM(page_table.shape, jnp.int32),
            pltpu.SMEM(lengths.shape, jnp.int32),
            pltpu.SMEM((slots, helpers), jnp.int32),
            pltpu.VMEM(counts.shape, jnp.int32),
            pltpu.VMEM(page_owner.shape[1:], jnp.int32),
            pltpu.VMEM((requests, head_dim), bf16),
            pltpu.VMEM((requests, head_dim), bf16),
            pltpu.VMEM((rows, head_dim), bf16),
            pltpu.VMEM((requests, group, head_dim), f32),
            pltpu.VMEM((pool, page, head_dim), bf16),
            pltpu.VMEM((pool, page, head_dim), bf16),
            pltpu.VMEM((helpers, stored, head_dim), bf16),
            pltpu.VMEM((helpers, head_dim, stored), bf16),
            pltpu.VMEM((helpers, stored, head_dim), bf16),
            pltpu.VMEM((helpers, slot_rows, head_dim), bf16),
            pltpu.VMEM((helpers, slot_rows, head_dim), bf16),
            pltpu.VMEM((helpers, slot_rows, head_dim), bf16),
            pltpu.VMEM((helpers, slot_rows, head_dim), bf16),
            pltpu.VMEM((helpers, 1, 128), f32),
            pltpu.VMEM((helpers, 1, 128), f32),
            pltpu.VMEM((helpers, 1, stored), f32),
            pltpu.VMEM((helpers * slot_rows // 128, 128), jnp.int32),
            pltpu.VMEM((rows, head_dim), f32),
            pltpu.VMEM((rows, head_dim), f32),
            pltpu.VMEM((helpers, slot_rows, stored), f32),
            pltpu.VMEM((helpers, slot_rows, stored), bf16),
            pltpu.VMEM((rows, helpers * slot_rows), bf16),
            pltpu.SemaphoreType.DMA((12,)),
            pltpu.SemaphoreType.DMA((helpers,)),
            pltpu.SemaphoreType.DMA((helpers,)),
            pltpu.SemaphoreType.DMA((helpers,)),
            pltpu.SemaphoreType.DMA((helpers,)),
            pltpu.SemaphoreType.DMA((helpers,)),
            pltpu.SemaphoreType.DMA((helpers,)),
        ],
        compiler_params=pltpu.CompilerParams(
            collective_id=0, has_side_effects=True, vmem_limit_bytes=56 * 1024 * 1024
        ),
        cost_estimate=pl.CostEstimate(
            flops=4 * helpers * slot_rows * stored * head_dim,
            bytes_accessed=24 * helpers * stored * head_dim // 4,
            transcendentals=2 * helpers * slot_rows * stored,
        ),
    )(
        page_table,
        lengths,
        query_list[0].T,
        counts,
        page_owner[0],
        queries.reshape(rows, head_dim),
        new_keys.reshape(requests, head_dim),
        new_values.reshape(requests, head_dim),
        cache_keys.reshape(pool, page, head_dim),
        cache_values.reshape(pool, page, head_dim),
        remote_keys.reshape(helpers, stored, head_dim),
        remote_values.reshape(helpers, stored, head_dim),
    )
    return attended.reshape(requests, group, head_dim)


def solution(mesh):
    return jax.shard_map(
        per_device,
        mesh=mesh,
        in_specs=(
            P("inst", "tp", None),
            P("inst", "tp", None),
            P("inst", "tp", None),
            P("inst", None, "tp", None),
            P("inst", None, "tp", None),
            P("inst", None),
            P("inst"),
            P("inst", None, "tp", None),
            P("inst", None, "tp", None),
            P("inst", None),
            P("inst", None, None),
            P("inst", None, None),
        ),
        out_specs=P("inst", "tp", None),
        check_vma=False,
    )
```
